32 devices in a mesh: gx: 4 (over x, core), gy: 8 (over z, y).
Axes of the slice: x: 2, y: 2, z: 4, core: 2. Of those that a mesh axis runs over, the one named last changes fastest.
Arguments:
- tokens: bfloat16 [16384, 1280], P(('gx', 'gy')), may hold values from -6 to 6
- out_grad: bfloat16 [16384, 1280], P(('gx', 'gy')), may hold values from -400 to 400
- segments: int32 [32, 512], P(('gx', 'gy')), may hold values from 0 to 7, never falling along the last dimension, each value on 1 to 256 neighbouring positions
- pos_rows: int32 [16384], P(('gx', 'gy')), may hold values from 0 to 15
- pos_cols: int32 [16384], P(('gx', 'gy')), may hold values from 0 to 15
- row_table: bfloat16 [16, 1280], replicated, may hold values from -4 to 4
- col_table: bfloat16 [16, 1280], replicated, may hold values from -4 to 4
- norm_gain: float32 [1280], replicated, may hold values from 0.25 to 1.75
- master_up: float32 [1280, 2560], P('gx'), may hold values from -0.15625 to 0.15625
- master_down: float32 [1280, 2560], P('gx'), may hold values from -0.125 to 0.125
- moment_up: float32 [1280, 2560], P('gx'), may hold values from -6 to 6
- moment_down: float32 [1280, 2560], P('gx'), may hold values from -6 to 6
Outputs:
- new_master_up: float32 [1280, 2560], P('gx')
- new_master_down: float32 [1280, 2560], P('gx')
- new_moment_up: float32 [1280, 2560], P('gx')
- new_moment_down: float32 [1280, 2560], P('gx')
The draws below stay inside these ranges and needn't reach their ends.
Inputs may be any that keep to these rules, and one draw needn't show every extreme that they name: `segments`: each replica's 512 tokens hold all 8 images in order, each of 1 to 256 tokens.
All inputs are finite; a program needn't handle non-finite values.
Results may differ from the reference program's by a relative error of at most 0.02.
Values may be sent and summed in bfloat16 or wider, within the bound.
A program may use at most 128 MiB of HBM per device.

```python
import math
import jax
import jax.numpy as jnp
import numpy as np
from jax import lax

D = 1280
FF = 2560
GRID = 16
IMGS = 8
TOK_DEV = 512
MOST = 256
TOKENS = 16384
N_GX = 4
N_GY = 8
DEVICES = 32


def draw_out_grad(key, part):
    first_key, second_key = jax.random.split(key, 2)
    feature = jnp.arange(D, dtype=jnp.float32) / D
    roughness = jax.random.uniform(second_key, (D,), minval=0.5, maxval=2.0)
    base = jnp.clip(jax.random.normal(first_key, (TOKENS, D)), -5.0, 5.0)
    rising = jnp.exp(jnp.log(3.0) * feature)
    values = base * rising[None, :] * roughness[None, :]
    return values.astype(jnp.bfloat16)


def set_ends(result, stream_key, low, high):
    place = [jax.random.randint(jax.random.fold_in(stream_key, axis), (), 0, length) for axis, length in enumerate(result.shape)]
    longest = result.shape.index(max(result.shape))
    neighbour = place[:longest] + [(place[longest] + 1) % result.shape[longest]] + place[longest + 1:]
    return result.at[tuple(place)].set(low).at[tuple(neighbour)].set(high)


def block_levels(stream_key, dims, cuts, least, largest):
    loudness = 1.0
    for axis_at, parts in cuts:
        heights = jax.random.uniform(jax.random.fold_in(jax.random.fold_in(stream_key, 6), axis_at), (parts,), jnp.float32, least / len(cuts), largest / len(cuts))
        loudness = loudness * jnp.repeat(jnp.exp(heights), dims[axis_at] // parts).reshape((-1,) + (1,) * (len(dims) - 1 - axis_at))
    return loudness


def split_up(number_of, total, reach, slope):
    weights = [(1 << 20) // math.isqrt(grade ** slope) + 1 for grade in range(2, number_of + 1)]
    spare, counts = total - reach - (number_of - 1), [1] * (number_of - 1)
    while spare > 0:
        candidates = [i for i in range(number_of - 1) if counts[i] < reach]
        whole, left = sum([weights[i] for i in candidates]), spare
        for i in candidates:
            extra = min(reach - counts[i], max(1, left * weights[i] // whole), spare)
            counts[i] = counts[i] + extra
            spare = spare - extra
    return np.array([reach] + counts)


def uneven_parts(key, number_of, total, limit, lean):
    if number_of == 2:
        one = jax.random.randint(key, (), max(1, total - limit), min(limit, total - 1) + 1)
        return jnp.stack([one, total - one])
    tallies = jnp.asarray(split_up(number_of, total, limit, lean), jnp.int32)
    twos = (number_of - 1) // 2
    donor, taker = tallies[1:1 + 2 * twos:2], tallies[2:2 + 2 * twos:2]
    margin = jnp.minimum(donor - 1, limit - taker)
    passed = jax.random.randint(jax.random.fold_in(key, 1), (twos,), 0, 1 << 20) % (margin + 1)
    tallies = tallies.at[1:1 + 2 * twos:2].set(donor - passed).at[2:2 + 2 * twos:2].set(taker + passed)
    return tallies[jax.random.permutation(jax.random.fold_in(key, 2), number_of)]


def bell_draw(key, dims, spread, most, cuts=(), kind=jnp.bfloat16):
    values = spread * jax.random.normal(key, dims, jnp.float32)
    if cuts:
        values = values * block_levels(key, dims, cuts, -0.22, 0.18)
    return jnp.clip(values, -most, most).astype(kind)


def setup_inputs(seed: int = 0) -> dict:
    key_of = jax.random.split(jax.random.key(seed), 13)
    return {
        "tokens": bell_draw(key_of[0], (TOKENS, D), 1.0, 6.0, ((0, 32),)),
        "out_grad": draw_out_grad(jax.random.fold_in(key_of[12], 71), 0),
        "segments": jax.vmap(lambda own: jnp.searchsorted(jnp.cumsum(uneven_parts(own, IMGS, TOK_DEV, MOST, 2)), jnp.arange(TOK_DEV), side="right"))(jax.random.split(key_of[2], DEVICES)).reshape((DEVICES, TOK_DEV)).astype(jnp.int32),
        "pos_rows": set_ends(jax.random.randint(key_of[3], (TOKENS,), 0, GRID), jax.random.fold_in(key_of[3], 1), 0, GRID - 1).astype(jnp.int32),
        "pos_cols": set_ends(jax.random.randint(key_of[4], (TOKENS,), 0, GRID), jax.random.fold_in(key_of[4], 1), 0, GRID - 1).astype(jnp.int32),
        "row_table": bell_draw(key_of[5], (GRID, D), 0.7, 4.0),
        "col_table": bell_draw(key_of[6], (GRID, D), 0.7, 4.0),
        "norm_gain": jnp.clip(1.0 + 0.15 * jax.random.normal(key_of[7], (D,), jnp.float32), 0.25, 1.75),
        "master_up": bell_draw(key_of[8], (D, FF), D ** -0.5, 0.15625, ((0, 4),), jnp.float32),
        "master_down": bell_draw(key_of[9], (D, FF), FF ** -0.5, 0.125, ((0, 4),), jnp.float32),
        "moment_up": bell_draw(key_of[10], (D, FF), 1.0, 6.0, ((0, 4),), jnp.float32),
        "moment_down": bell_draw(key_of[11], (D, FF), 1.0, 6.0, ((0, 4),), jnp.float32),
    }


momentum_keep = 0.9
learn_rate = 0.01

def gelu_tanh(values):
    return 0.5 * values * (1.0 + jnp.tanh(0.7978845608 * (values + 0.044715 * values * values * values)))

def table_lookup(positions, table):
    onehot = (positions[:, None] == jnp.arange(GRID, dtype=jnp.int32)[None, :]).astype(jnp.bfloat16)
    return jnp.dot(onehot, table, preferred_element_type=jnp.float32)

def replica_grads(tok_rows, grad_rows, seg_row, row_ids, col_ids, row_table, col_table, norm_gain, w_up, w_down):
    embedded = tok_rows.astype(jnp.float32) + table_lookup(row_ids, row_table) + table_lookup(col_ids, col_table)
    average = lax.optimization_barrier(jnp.mean(embedded, axis=1, keepdims=True))
    centered = embedded - average
    variance = lax.optimization_barrier(jnp.mean(centered * centered, axis=1, keepdims=True))
    normed = (centered * lax.rsqrt(variance + 1e-06) * norm_gain[None, :]).astype(jnp.bfloat16)
    pre_act = jnp.dot(normed, w_up, preferred_element_type=jnp.float32)
    hidden = gelu_tanh(pre_act).astype(jnp.bfloat16)
    member = (seg_row[:, None] == jnp.arange(IMGS, dtype=jnp.int32)[None, :]).astype(jnp.float32)
    per_image = 1.0 / lax.optimization_barrier(jnp.sum(member, axis=0))
    token_weight = jnp.dot(member, per_image)
    weighted = (grad_rows.astype(jnp.float32) * token_weight[:, None]).astype(jnp.bfloat16)
    hidden_grad = jnp.dot(weighted, w_down, preferred_element_type=jnp.float32)
    _, backward = jax.vjp(gelu_tanh, pre_act)
    pre_grad = backward(hidden_grad)[0].astype(jnp.bfloat16)
    grad_up = lax.dot_general(normed, pre_grad, (((0,), (0,)), ((), ())), preferred_element_type=jnp.float32)
    grad_down = lax.dot_general(weighted, hidden, (((0,), (0,)), ((), ())), preferred_element_type=jnp.float32)
    return jnp.concatenate([grad_up.astype(jnp.bfloat16), grad_down.astype(jnp.bfloat16)], axis=1)

def reference(tokens, out_grad, segments, pos_rows, pos_cols, row_table, col_table, norm_gain, master_up, master_down, moment_up, moment_down):
    w_up = master_up.astype(jnp.bfloat16)
    w_down = master_down.astype(jnp.bfloat16)
    replicas = N_GX * N_GY

    def accumulate(running, replica):
        first = (replica * TOK_DEV).astype(jnp.int32)
        tok_rows = lax.dynamic_slice_in_dim(tokens, first, TOK_DEV, 0)
        grad_rows = lax.dynamic_slice_in_dim(out_grad, first, TOK_DEV, 0)
        row_ids = lax.dynamic_slice_in_dim(pos_rows, first, TOK_DEV, 0)
        col_ids = lax.dynamic_slice_in_dim(pos_cols, first, TOK_DEV, 0)
        seg_row = lax.dynamic_slice_in_dim(segments, replica.astype(jnp.int32), 1, 0)[0]
        grads = replica_grads(tok_rows, grad_rows, seg_row, row_ids, col_ids, row_table, col_table, norm_gain, w_up, w_down)
        return (running + grads.astype(jnp.float32), None)
    start_sum = jnp.zeros((D, 2 * FF), jnp.float32)
    grad_sum, _ = lax.scan(accumulate, start_sum, jnp.arange(replicas, dtype=jnp.int32))
    scale = lax.rsqrt(jnp.mean(grad_sum * grad_sum) + 1e-06)
    moments = jnp.concatenate([moment_up, moment_down], axis=1)
    masters = jnp.concatenate([master_up, master_down], axis=1)
    new_moments = momentum_keep * moments + scale * grad_sum
    new_masters = masters - learn_rate * new_moments
    return (new_masters[:, :FF], new_masters[:, FF:], new_moments[:, :FF], new_moments[:, FF:])
```

```python
import functools

import jax
import jax.numpy as jnp
from jax import lax
from jax.experimental import pallas as pl
from jax.experimental.pallas import tpu as pltpu
from jax.sharding import PartitionSpec as P

momentum_keep = 0.9
learn_rate = 0.01
MESH = pl.DeviceIdType.MESH
VMEM = pltpu.VMEM
VMEM_LIMIT = 60 * 1024 * 1024
CORES = 2
PAIR = 2
PARTS = 2
Q = 2
S = 4


def gelu_tanh(values):
    return (
        0.5
        * values
        * (1.0 + jnp.tanh(0.7978845608 * (values + 0.044715 * values * values * values)))
    )


class Copies:
    def __init__(self, send, recv):
        self.send, self.recv, self.count, self.all = send, recv, 0, []

    def start(self, src, dst, device):
        copy = pltpu.make_async_remote_copy(
            src_ref=src,
            dst_ref=dst,
            send_sem=self.send.at[self.count],
            recv_sem=self.recv.at[self.count],
            device_id=device,
            device_id_type=MESH,
        )
        copy.start()
        self.count += 1
        self.all.append(copy)
        return copy

    def finish(self):
        for copy in self.all:
            copy.wait_send()


def greet(devices):
    barrier = pltpu.get_barrier_semaphore()
    for device in devices:
        pl.semaphore_signal(barrier, inc=1, device_id=device, device_id_type=MESH)
    pl.semaphore_wait(barrier, len(devices))


def place():
    gx, gy = lax.axis_index("gx"), lax.axis_index("gy")
    return gx, gy, gx // CORES, lax.rem(gx, CORES), gy // PAIR, lax.rem(gy, PAIR)


def gather_kernel(
    shard, tokens, out_grad, seg, rows, cols, table, gain, full, normed, weighted, send, recv
):
    gx, gy, x, c, h, l = place()
    partner = (x * CORES + 1 - c, gy)
    across = ((1 - x) * CORES + c, gy)
    diagonal = ((1 - x) * CORES + 1 - c, gy)
    beside = (gx, h * PAIR + 1 - l)
    greet([partner, across, diagonal, beside])
    copies = Copies(send, recv)
    depth = shard.shape[2]
    step = depth // S
    straight, crossed = [], []
    for s in range(S):
        part = pl.ds(s * step, step)
        straight.append(
            copies.start(shard.at[c, l, part], full.at[l, gx, part], across)
        )
        crossed.append(
            copies.start(shard.at[1 - c, l, part], full.at[l, gx, part], diagonal)
        )
    near = [copies.start(shard.at[1 - c, u], full.at[u, gx], partner) for u in range(PARTS)]
    for u in range(PARTS):
        full[u, gx] = shard[c, u]

    count = tokens.shape[0]
    grid = table.shape[0] // 2
    lanes = lax.broadcasted_iota(jnp.int32, (count, 128), 1)
    sizes = jnp.sum((seg[...] == lanes).astype(jnp.float32), axis=0, keepdims=True)
    per_image = 1.0 / jnp.maximum(sizes, 1.0)
    tile = 64

    @pl.loop(0, count // tile)
    def _(i):
        own = pl.ds(pl.multiple_of(i * tile, tile), tile)
        hot = lax.broadcasted_iota(jnp.int32, (tile, 2 * grid), 1)
        hot = ((hot == rows[own, :]) | (hot == cols[own, :] + grid)).astype(jnp.float32)
        embedded = tokens[own, :].astype(jnp.float32) + jnp.dot(
            hot.astype(jnp.bfloat16), table[...], preferred_element_type=jnp.float32
        )
        average = jnp.mean(embedded, axis=1, keepdims=True)
        centered = embedded - average
        variance = jnp.mean(centered * centered, axis=1, keepdims=True)
        normed[c, own, :] = (centered * lax.rsqrt(variance + 1e-06) * gain[...]).astype(
            jnp.bfloat16
        )
        lane = lax.broadcasted_iota(jnp.int32, (tile, 128), 1)
        member = (seg[own, :] == lane).astype(jnp.float32)
        weight = jnp.sum(member * per_image, axis=1, keepdims=True)
        weighted[c, own, :] = (out_grad[own, :].astype(jnp.float32) * weight).astype(jnp.bfloat16)

    shared = [
        copies.start(normed.at[c], normed.at[c], partner),
        copies.start(weighted.at[c], weighted.at[c], partner),
    ]
    passed = []
    for s in range(S):
        part = pl.ds(s * step, step)
        for arrived, owner in ((straight[s], across[0]), (crossed[s], diagonal[0])):
            arrived.wait_recv()
            piece = full.at[l, owner, part]
            passed.append(copies.start(piece, piece, beside))
    for copy in near + shared + passed:
        copy.wait_recv()
    copies.finish()


def reduce_kernel(
    norm_t, weight_t, pre_grad, hidden, out, squares,
    s1, r1, keep, s2, r2, s3, r3, whole, ss, ss_s, ss_r, send, recv,
):
    gx, gy, x, c, h, l = place()
    levels = lax.axis_size("gy") // PAIR
    partner = (x * CORES + 1 - c, gy)
    across = ((1 - x) * CORES + c, gy)
    beside = (gx, h * PAIR + 1 - l)
    ahead = [lax.rem(h + k, levels) for k in range(levels)]
    behind = [lax.rem(h + levels - k, levels) for k in range(levels)]
    above = [(gx, ahead[k] * PAIR + l) for k in range(levels)]
    greet([partner, across, beside] + above[1:])
    copies = Copies(send, recv)
    lefts, rights = (norm_t, weight_t), (pre_grad, hidden)
    block, width = s1.shape[3], s1.shape[4]
    deep = block // levels

    def product(p, q, at_x, at_l):
        own = pl.ds(pl.multiple_of((at_x * PAIR + at_l) * block, 16), block)
        return jnp.dot(
            lefts[p][own, :],
            rights[p][:, q * width : (q + 1) * width],
            preferred_element_type=jnp.float32,
        )

    first = {}
    targets = (across, beside)
    for q in range(Q):
        for slot in range(2):
            for p in range(PARTS):
                at = (1 - x, 1 - l) if slot == 0 else ((1 - x, l), (x, 1 - l))[p]
                s1[q, p, slot] = product(p, q, *at).astype(jnp.bfloat16)
                first[q, p, slot] = copies.start(
                    s1.at[q, p, slot], r1.at[q, p, slot], targets[p]
                )
    for q in range(Q):
        for slot in range(2):
            for p in range(PARTS):
                at = (x, l) if slot == 1 else ((x, 1 - l), (1 - x, l))[p]
                keep[q, p, slot] = product(p, q, *at)

    second = {}
    for q in range(Q):
        for p in range(PARTS):
            first[q, p, 0].wait_recv()
            s2[q, p] = (keep[q, p, 0] + r1[q, p, 0].astype(jnp.float32)).astype(jnp.bfloat16)
            second[q, p] = copies.start(s2.at[q, p], r2.at[q, p], targets[1 - p])

    third = {}
    for q in range(Q):
        for p in range(PARTS):
            first[q, p, 1].wait_recv()
            second[q, p].wait_recv()
            total = (
                keep[q, p, 1] + r1[q, p, 1].astype(jnp.float32) + r2[q, p].astype(jnp.float32)
            )
            keep[q, p, 1] = total
            for level in range(levels):
                s3[q, level, p] = total[level * deep : (level + 1) * deep].astype(jnp.bfloat16)
        for k in range(1, levels):
            third[q, k] = copies.start(s3.at[q, ahead[k]], r3.at[q, h], above[k])

    spread, passed = {}, []
    ss[...] = jnp.zeros_like(ss)
    mine = pl.ds(pl.multiple_of(h * deep, 16), deep)
    for q in range(Q):
        for k in range(1, levels):
            third[q, k].wait_recv()
        for p in range(PARTS):
            total = keep[q, p, 1, mine, :]
            for k in range(1, levels):
                total = total + r3[q, behind[k], p].astype(jnp.float32)
            whole[l, q, h, p] = total.astype(jnp.bfloat16)
            power = jnp.sum((total * total).reshape(deep // 8, 8, width), axis=0)
            for lane in range(width // 128):
                ss[...] += power[:, lane * 128 : (lane + 1) * 128]
        piece = whole.at[l, q, h]
        for k in range(1, levels):
            spread[q, k] = copies.start(piece, piece, above[k])
        passed.append(copies.start(piece, piece, beside))

    ss_s[0] = ss[...]
    waits = [copies.start(ss_s.at[0], ss_r.at[h], above[k]) for k in range(1, levels)]
    ss_r[h] = ss[...]
    for copy in waits:
        copy.wait_recv()
    running = ss_r[0]
    for level in range(1, levels):
        running = running + ss_r[level]
    for turn, target in enumerate((beside, across, partner)):
        ss_s[1 + turn] = running
        copies.start(ss_s.at[1 + turn], ss_r.at[levels + turn], target).wait_recv()
        running = running + ss_r[levels + turn]
    squares[...] = running

    for q in range(Q):
        for k in range(1, levels):
            spread[q, k].wait_recv()
            piece = whole.at[l, q, behind[k]]
            passed.append(copies.start(piece, piece, beside))
    for copy in passed:
        copy.wait_recv()
    last = [copies.start(whole.at[1 - c, q], out.at[c, q], partner) for q in range(Q)]
    for q in range(Q):
        out[c, q] = whole[c, q]
    for copy in last:
        copy.wait_recv()
    copies.finish()


def update_kernel(
    entries, grads, squares, up, down, moment_up, moment_down, new_up, new_down, new_mu, new_md
):
    scale = lax.rsqrt(jnp.sum(squares[...]) / entries + 1e-06)
    width = grads.shape[5]
    for q in range(Q):
        at = slice(q * width, (q + 1) * width)
        for p, old, moment, new, new_moment in (
            (0, up, moment_up, new_up, new_mu),
            (1, down, moment_down, new_down, new_md),
        ):
            fresh = momentum_keep * moment[:, at] + scale * grads[0, q, 0, p].astype(jnp.float32)
            new_moment[:, at] = fresh
            new[:, at] = old[:, at] - learn_rate * fresh


def cost(flops, moved):
    return pl.CostEstimate(flops=flops, bytes_accessed=moved, transcendentals=0)


def kernel_plan(
    tokens, out_grad, segments, pos_rows, pos_cols, row_table, col_table, norm_gain,
    master_up, master_down, moment_up, moment_down,
):
    bf16, f32 = jnp.bfloat16, jnp.float32
    shape = jax.ShapeDtypeStruct
    count, width = tokens.shape
    depth, hidden_units = master_up.shape
    gx, gy = lax.axis_size("gx"), lax.axis_size("gy")
    levels = gy // PAIR
    half = hidden_units // CORES
    shard = jnp.stack(
        [
            jnp.stack([m[:, i * half : (i + 1) * half].astype(bf16) for m in (master_up, master_down)])
            for i in range(CORES)
        ]
    )
    vm = pl.BlockSpec(memory_space=VMEM)
    n_copies = 4 * S + 4
    full, normed, weighted = pl.pallas_call(
        gather_kernel,
        out_shape=(
            shape((PARTS, gx, depth, half), bf16),
            shape((CORES, count, width), bf16),
            shape((CORES, count, width), bf16),
        ),
        in_specs=[vm] * 8,
        out_specs=(vm, vm, vm),
        scratch_shapes=[
            pltpu.SemaphoreType.DMA((n_copies,)),
            pltpu.SemaphoreType.DMA((n_copies,)),
        ],
        cost_estimate=cost(0, 4 * shard.size),
        compiler_params=pltpu.CompilerParams(
            collective_id=0, has_side_effects=True, vmem_limit_bytes=VMEM_LIMIT
        ),
    )(
        shard,
        tokens,
        out_grad,
        segments.reshape(count, 1),
        pos_rows.reshape(count, 1),
        pos_cols.reshape(count, 1),
        jnp.concatenate([row_table, col_table], axis=0),
        norm_gain.reshape(1, width),
    )
    both = CORES * count
    normed = normed.reshape(both, width)
    weighted = weighted.reshape(both, width)
    full = full.reshape(PARTS, width, half)
    pre_act = jnp.dot(normed, full[0], preferred_element_type=f32)
    hidden, backward = jax.vjp(gelu_tanh, pre_act)
    hidden_grad = jnp.dot(weighted, full[1], preferred_element_type=f32)
    pre_grad = backward(hidden_grad)[0].astype(bf16)
    hidden = hidden.astype(bf16)

    block = width // (gx // CORES) // PAIR
    cols = half // Q
    deep = block // levels
    n_copies = Q * (6 + 2 * (levels - 1) + levels + 1) + levels + 2
    grads, squares = pl.pallas_call(
        reduce_kernel,
        out_shape=(shape((CORES, Q, levels, PARTS, deep, cols), bf16), shape((8, 128), f32)),
        in_specs=[vm] * 4,
        out_specs=(vm, vm),
        scratch_shapes=[
            VMEM((Q, PARTS, 2, block, cols), bf16),
            VMEM((Q, PARTS, 2, block, cols), bf16),
            VMEM((Q, PARTS, 2, block, cols), f32),
            VMEM((Q, PARTS, block, cols), bf16),
            VMEM((Q, PARTS, block, cols), bf16),
            VMEM((Q, levels, PARTS, deep, cols), bf16),
            VMEM((Q, levels, PARTS, deep, cols), bf16),
            VMEM((PAIR, Q, levels, PARTS, deep, cols), bf16),
            VMEM((8, 128), f32),
            VMEM((4, 8, 128), f32),
            VMEM((levels + 3, 8, 128), f32),
            pltpu.SemaphoreType.DMA((n_copies,)),
            pltpu.SemaphoreType.DMA((n_copies,)),
        ],
        cost_estimate=cost(4 * both * width * half, 8 * both * width),
        compiler_params=pltpu.CompilerParams(
            collective_id=1, has_side_effects=True, vmem_limit_bytes=VMEM_LIMIT
        ),
    )(normed.T, weighted.T, pre_grad, hidden)

    flat = pl.BlockSpec((deep, half), lambda i, j: (i, j))
    return pl.pallas_call(
        functools.partial(update_kernel, 2.0 * width * hidden_units),
        grid=(levels, CORES),
        out_shape=(shape(master_up.shape, f32),) * 4,
        in_specs=[
            pl.BlockSpec((1, Q, 1, PARTS, deep, cols), lambda i, j: (j, 0, i, 0, 0, 0)),
            pl.BlockSpec((8, 128), lambda i, j: (0, 0)),
            flat, flat, flat, flat,
        ],
        out_specs=(flat,) * 4,
        cost_estimate=cost(8 * master_up.size, 34 * master_up.size),
        compiler_params=pltpu.CompilerParams(vmem_limit_bytes=VMEM_LIMIT),
    )(grads, squares, master_up, master_down, moment_up, moment_down)


def table_lookup(positions, table):
    onehot = (
        positions[:, None] == jnp.arange(table.shape[0], dtype=jnp.int32)[None, :]
    ).astype(jnp.bfloat16)
    return jnp.dot(onehot, table, preferred_element_type=jnp.float32)


def column_product(left, right):
    return lax.dot_general(
        left, right, (((0,), (0,)), ((), ())), preferred_element_type=jnp.float32
    )


def collective_plan(
    tokens, out_grad, segments, pos_rows, pos_cols, row_table, col_table, norm_gain,
    master_up, master_down, moment_up, moment_down,
):
    images = 8
    embedded = (
        tokens.astype(jnp.float32)
        + table_lookup(pos_rows, row_table)
        + table_lookup(pos_cols, col_table)
    )
    average = jnp.mean(embedded, axis=1, keepdims=True)
    centered = embedded - average
    variance = jnp.mean(centered * centered, axis=1, keepdims=True)
    normed = (centered * lax.rsqrt(variance + 1e-06) * norm_gain[None, :]).astype(jnp.bfloat16)
    member = (segments[0][:, None] == jnp.arange(images, dtype=jnp.int32)[None, :]).astype(
        jnp.float32
    )
    token_weight = jnp.dot(member, 1.0 / jnp.sum(member, axis=0))
    weighted = (out_grad.astype(jnp.float32) * token_weight[:, None]).astype(jnp.bfloat16)
    w_up = lax.all_gather(master_up.astype(jnp.bfloat16), "gx", axis=0, tiled=True)
    pre_act = jnp.dot(normed, w_up, preferred_element_type=jnp.float32)
    hidden, backward = jax.vjp(gelu_tanh, pre_act)
    w_down = lax.all_gather(master_down.astype(jnp.bfloat16), "gx", axis=0, tiled=True)
    hidden_grad = jnp.dot(weighted, w_down, preferred_element_type=jnp.float32)
    pre_grad = backward(hidden_grad)[0].astype(jnp.bfloat16)
    grads = [column_product(normed, pre_grad), column_product(weighted, hidden.astype(jnp.bfloat16))]
    group_sum = lax.psum_scatter(
        jnp.concatenate(grads, axis=1).astype(jnp.bfloat16), "gx", scatter_dimension=0, tiled=True
    )
    grad_sum = lax.psum(group_sum, "gy").astype(jnp.float32)
    squares = lax.psum(jnp.sum(grad_sum * grad_sum), "gx")
    entries = 2.0 * tokens.shape[1] * master_up.shape[1]
    scale = lax.rsqrt(squares / entries + 1e-06)
    half = master_up.shape[1]
    new_mu = momentum_keep * moment_up + scale * grad_sum[:, :half]
    new_md = momentum_keep * moment_down + scale * grad_sum[:, half:]
    return master_up - learn_rate * new_mu, master_down - learn_rate * new_md, new_mu, new_md


def solution(mesh):
    gx, gy = mesh.shape["gx"], mesh.shape["gy"]

    def on_device(*args):
        width, half = args[0].shape[1], args[8].shape[1] // CORES
        fits = (
            gx == 2 * CORES
            and gy % PAIR == 0
            and gy > PAIR
            and width % (gx * gy // CORES * 16) == 0
            and width % (gx * S * 16) == 0
            and half % (Q * 128) == 0
        )
        return (kernel_plan if fits else collective_plan)(*args)

    both, rows = P(("gx", "gy"), None), P("gx", None)
    return jax.shard_map(
        on_device,
        mesh=mesh,
        in_specs=(both, both, both, P(("gx", "gy")), P(("gx", "gy")), P(), P(), P())
        + (rows,) * 4,
        out_specs=(rows,) * 4,
        check_vma=False,
    )
```

```python
import functools

import jax
import jax.numpy as jnp
from jax import lax
from jax.experimental import pallas as pl
from jax.experimental.pallas import tpu as pltpu
from jax.sharding import PartitionSpec as P

momentum_keep = 0.9
learn_rate = 0.01
MESH = pl.DeviceIdType.MESH
VMEM = pltpu.VMEM
VMEM_LIMIT = 60 * 1024 * 1024
CORES = 2
PAIR = 2
PARTS = 2
Q = 5


def gelu_tanh(values):
    return (
        0.5
        * values
        * (1.0 + jnp.tanh(0.7978845608 * (values + 0.044715 * values * values * values)))
    )


class Copies:
    def __init__(self, send, recv):
        self.send, self.recv, self.count, self.all = send, recv, 0, []

    def start(self, src, dst, device):
        copy = pltpu.make_async_remote_copy(
            src_ref=src,
            dst_ref=dst,
            send_sem=self.send.at[self.count],
            recv_sem=self.recv.at[self.count],
            device_id=device,
            device_id_type=MESH,
        )
        copy.start()
        self.count += 1
        self.all.append(copy)
        return copy

    def finish(self):
        for copy in self.all:
            copy.wait_send()


def greet(devices):
    barrier = pltpu.get_barrier_semaphore()
    for device in devices:
        pl.semaphore_signal(barrier, inc=1, device_id=device, device_id_type=MESH)
    pl.semaphore_wait(barrier, len(devices))


def place():
    gx, gy = lax.axis_index("gx"), lax.axis_index("gy")
    return gx, gy, gx // CORES, lax.rem(gx, CORES), gy // PAIR, lax.rem(gy, PAIR)


def block_kernel(
    master_up, master_down, tokens, out_grad, seg, rows, cols, row_table, col_table, gain,
    out, squares,
    shard, full, normed, weighted, norm_t, weight_t, pre_grad, hidden,
    s1, r1, s2, r2, s3, r3, keep, whole, ss, ss_s, ss_r, send, recv,
):
    bf16, f32 = jnp.bfloat16, jnp.float32
    gx, gy, x, c, h, l = place()
    levels = lax.axis_size("gy") // PAIR
    partner = (x * CORES + 1 - c, gy)
    across = ((1 - x) * CORES + c, gy)
    diagonal = ((1 - x) * CORES + 1 - c, gy)
    beside = (gx, h * PAIR + 1 - l)
    odd = lax.rem(h, 2)
    neighbour = (gx, (h + 1 - 2 * odd) * PAIR + l)
    ahead = [lax.rem(h + k, levels) for k in range(levels)]
    behind = [lax.rem(h + levels - k, levels) for k in range(levels)]
    above = [(gx, ahead[k] * PAIR + l) for k in range(levels)]
    greet([partner, across, diagonal, beside] + above[1:])
    copies = Copies(send, recv)
    chunks, depth, width = shard.shape[1], shard.shape[3], shard.shape[4]
    count, features = tokens.shape
    block = s1.shape[3]
    deep = block // levels

    straight, crossed, near, passed = {}, {}, {}, {}

    def send_weights(q):
        for k in range(CORES):
            at = slice((k * chunks + q) * width, (k * chunks + q + 1) * width)
            shard[k, q, 0] = master_up[:, at].astype(bf16)
            shard[k, q, 1] = master_down[:, at].astype(bf16)
        mine = full.at[q, odd, gx]
        straight[q] = copies.start(shard.at[c, q, odd], mine, across)
        crossed[q] = copies.start(shard.at[1 - c, q, odd], mine, diagonal)
        near[q] = copies.start(shard.at[1 - c, q], full.at[q, :, gx], partner)
        for u in range(PARTS):
            full[q, u, gx] = shard[c, q, u]

    def pass_weights(q):
        for k, (arrived, owner) in enumerate(((straight[q], across[0]), (crossed[q], diagonal[0]))):
            arrived.wait_recv()
            piece = full.at[q, odd, owner]
            passed[q, k] = copies.start(piece, piece, neighbour)

    def column(row, lanes):
        return jnp.broadcast_to(row, (lanes, row.shape[1])).T

    def layer_norm():
        grid, tile = row_table.shape[0], 128
        images = lax.broadcasted_iota(jnp.int32, (128, count), 0)
        member = (jnp.broadcast_to(seg[...], (128, count)) == images).astype(f32)
        sizes = jnp.maximum(jnp.sum(member, axis=1, keepdims=True), 1.0)
        token_weight = jnp.sum(member * (1.0 / sizes), axis=0, keepdims=True)
        places = lax.broadcasted_iota(jnp.int32, (tile, 128), 1)
        for i in range(count // tile):
            at = slice(i * tile, (i + 1) * tile)
            own = pl.ds(pl.multiple_of(c * count + i * tile, tile), tile)
            embedded = tokens[at, :].astype(f32)
            for index, table in ((rows, row_table), (cols, col_table)):
                hot = column(index[:, at].astype(f32), 128)[:, :grid] == places[:, :grid].astype(f32)
                embedded += jnp.dot(
                    hot.astype(f32).astype(bf16), table[...], preferred_element_type=f32
                )
            average = jnp.mean(embedded, axis=1, keepdims=True)
            centered = embedded - average
            variance = jnp.mean(centered * centered, axis=1, keepdims=True)
            left = (centered * lax.rsqrt(variance + 1e-06) * gain[...]).astype(bf16)
            normed[own, :] = left
            norm_t[c, :, at] = left.T
            weight = column(token_weight[:, at], 128)[:, :1]
            right = (out_grad[at, :].astype(f32) * weight).astype(bf16)
            weighted[own, :] = right
            weight_t[c, :, at] = right.T

    def forward(q):
        near[q].wait_recv()
        for k in range(2):
            passed[q, k].wait_recv()
        up = full.at[q, 0]
        down = full.at[q, 1]
        tile = 256
        total = CORES * count

        @pl.loop(0, total // tile)
        def _(i):
            own = pl.ds(pl.multiple_of(i * tile, tile), tile)
            v = jnp.dot(
                normed[own, :], up[...].reshape(features, width), preferred_element_type=f32
            )
            grad = jnp.dot(
                weighted[own, :], down[...].reshape(features, width), preferred_element_type=f32
            )
            square = v * v
            t = jnp.tanh(0.7978845608 * (v + 0.044715 * (square * v)))
            rising = 0.5 * (1.0 + t)
            slope = 0.7978845608 * (1.0 + 3.0 * 0.044715 * square)
            hidden[q, own, :] = (v * rising).astype(bf16)
            pre_grad[q, own, :] = (grad * (rising + 0.5 * v * (1.0 - t * t) * slope)).astype(bf16)

    def product(p, q, at_x, at_l):
        own = pl.ds(pl.multiple_of((at_x * PAIR + at_l) * block, 16), block)
        left, right = ((norm_t, pre_grad), (weight_t, hidden))[p]
        return sum(
            jnp.dot(
                left[k, own, :],
                right[q, k * count : (k + 1) * count, :],
                preferred_element_type=f32,
            )
            for k in range(CORES)
        )

    first, second, third, spread, beyond, last = {}, {}, {}, {}, {}, {}
    targets = (across, beside)

    def send_first(q):
        for slot in range(2):
            for p in range(PARTS):
                at = (1 - x, 1 - l) if slot == 0 else ((1 - x, l), (x, 1 - l))[p]
                s1[q, p, slot] = product(p, q, *at).astype(bf16)
                first[q, p, slot] = copies.start(
                    s1.at[q, p, slot], r1.at[q, p, slot], targets[p]
                )

    def send_second(q):
        for p in range(PARTS):
            own = product(p, q, *((x, 1 - l), (1 - x, l))[p])
            first[q, p, 0].wait_recv()
            s2[q, p] = (own + r1[q, p, 0].astype(f32)).astype(bf16)
            second[q, p] = copies.start(s2.at[q, p], r2.at[q, p], targets[1 - p])

    def send_third(q):
        for p in range(PARTS):
            own = product(p, q, x, l)
            first[q, p, 1].wait_recv()
            second[q, p].wait_recv()
            total = own + r1[q, p, 1].astype(f32) + r2[q, p].astype(f32)
            for level in range(levels):
                piece = total[level * deep : (level + 1) * deep]
                keep[q, level, p] = piece
                s3[q, level, p] = piece.astype(bf16)
        for k in range(1, levels):
            third[q, k] = copies.start(s3.at[q, ahead[k]], r3.at[q, h], above[k])

    def send_whole(q):
        for k in range(1, levels):
            third[q, k].wait_recv()
        for p in range(PARTS):
            total = keep[q, h, p]
            for k in range(1, levels):
                total = total + r3[q, behind[k], p].astype(f32)
            whole[l, q, h, p] = total.astype(bf16)
            power = jnp.sum((total * total).reshape(deep // 8, 8, width), axis=0)
            for lane in range(width // 128):
                ss[...] += power[:, lane * 128 : (lane + 1) * 128]
        piece = whole.at[l, q, h]
        for k in range(1, levels):
            spread[q, k] = copies.start(piece, piece, above[k])
        beyond[q, 0] = copies.start(piece, piece, beside)

    def pass_whole(q):
        for k in range(1, levels):
            spread[q, k].wait_recv()
            piece = whole.at[l, q, behind[k]]
            beyond[q, k] = copies.start(piece, piece, beside)

    def send_last(q):
        for k in range(levels):
            beyond[q, k].wait_recv()
        last[q] = copies.start(whole.at[1 - c, q], out.at[c, q], partner)
        out[c, q] = whole[c, q]

    def add_squares():
        ss_s[0] = ss[...]
        waits = [copies.start(ss_s.at[0], ss_r.at[h], above[k]) for k in range(1, levels)]
        ss_r[h] = ss[...]
        for copy in waits:
            copy.wait_recv()
        running = ss_r[0]
        for level in range(1, levels):
            running = running + ss_r[level]
        for turn, target in enumerate((beside, across, partner)):
            ss_s[1 + turn] = running
            copies.start(ss_s.at[1 + turn], ss_r.at[levels + turn], target).wait_recv()
            running = running + ss_r[levels + turn]
        squares[...] = running

    ss[...] = jnp.zeros_like(ss)
    send_weights(0)
    send_weights(1)
    layer_norm()
    mine = pl.ds(pl.multiple_of(c * count, 128), count)
    shared = [
        copies.start(piece, piece, partner)
        for piece in (normed.at[mine], weighted.at[mine], norm_t.at[c], weight_t.at[c])
    ]
    pass_weights(0)
    for copy in shared:
        copy.wait_recv()
    for tick in range(chunks + 5):
        if tick + 2 < chunks:
            send_weights(tick + 2)
        if tick + 1 < chunks:
            pass_weights(tick + 1)
        steps = (forward, send_first), (send_second,), (send_third,), (send_whole,), (pass_whole,), (send_last,)
        for lag, actions in enumerate(steps):
            if 0 <= tick - lag < chunks:
                for action in actions:
                    action(tick - lag)
        if tick == chunks + 2:
            add_squares()
    for q in range(chunks):
        last[q].wait_recv()
    copies.finish()


def update_kernel(
    entries, grads, squares, up, down, moment_up, moment_down, new_up, new_down, new_mu, new_md
):
    scale = lax.rsqrt(jnp.sum(squares[...]) / entries + 1e-06)
    width = grads.shape[5]
    for q in range(Q):
        at = slice(q * width, (q + 1) * width)
        for p, old, moment, new, new_moment in (
            (0, up, moment_up, new_up, new_mu),
            (1, down, moment_down, new_down, new_md),
        ):
            fresh = momentum_keep * moment[:, at] + scale * grads[0, q, 0, p].astype(jnp.float32)
            new_moment[:, at] = fresh
            new[:, at] = old[:, at] - learn_rate * fresh


def cost(flops, moved):
    return pl.CostEstimate(flops=flops, bytes_accessed=moved, transcendentals=0)


def kernel_plan(
    tokens, out_grad, segments, pos_rows, pos_cols, row_table, col_table, norm_gain,
    master_up, master_down, moment_up, moment_down,
):
    bf16, f32 = jnp.bfloat16, jnp.float32
    shape = jax.ShapeDtypeStruct
    count, width = tokens.shape
    depth, hidden_units = master_up.shape
    gx, gy = lax.axis_size("gx"), lax.axis_size("gy")
    levels = gy // PAIR
    half = hidden_units // CORES
    both = CORES * count
    block = width // (gx // CORES) // PAIR
    cols = half // Q
    deep = block // levels
    vm = pl.BlockSpec(memory_space=VMEM)
    n_copies = Q * (11 + 2 * (levels - 1) + levels + 1) + 4 + levels + 2
    grads, squares = pl.pallas_call(
        block_kernel,
        out_shape=(shape((CORES, Q, levels, PARTS, deep, cols), bf16), shape((8, 128), f32)),
        in_specs=[vm] * 10,
        out_specs=(vm, vm),
        scratch_shapes=[
            VMEM((CORES, Q, PARTS, depth, cols), bf16),
            VMEM((Q, PARTS, gx, depth, cols), bf16),
            VMEM((both, width), bf16),
            VMEM((both, width), bf16),
            VMEM((CORES, width, count), bf16),
            VMEM((CORES, width, count), bf16),
            VMEM((Q, both, cols), bf16),
            VMEM((Q, both, cols), bf16),
            VMEM((Q, PARTS, 2, block, cols), bf16),
            VMEM((Q, PARTS, 2, block, cols), bf16),
            VMEM((Q, PARTS, block, cols), bf16),
            VMEM((Q, PARTS, block, cols), bf16),
            VMEM((Q, levels, PARTS, deep, cols), bf16),
            VMEM((Q, levels, PARTS, deep, cols), bf16),
            VMEM((Q, levels, PARTS, deep, cols), f32),
            VMEM((PAIR, Q, levels, PARTS, deep, cols), bf16),
            VMEM((8, 128), f32),
            VMEM((4, 8, 128), f32),
            VMEM((levels + 3, 8, 128), f32),
            pltpu.SemaphoreType.DMA((n_copies,)),
            pltpu.SemaphoreType.DMA((n_copies,)),
        ],
        cost_estimate=cost(8 * both * width * half, 8 * both * width),
        compiler_params=pltpu.CompilerParams(
            collective_id=0, has_side_effects=True, vmem_limit_bytes=VMEM_LIMIT
        ),
    )(
        master_up,
        master_down,
        tokens,
        out_grad,
        segments,
        pos_rows.reshape(1, count),
        pos_cols.reshape(1, count),
        row_table,
        col_table,
        norm_gain.reshape(1, width),
    )

    flat = pl.BlockSpec((deep, half), lambda i, j: (i, j))
    return pl.pallas_call(
        functools.partial(update_kernel, 2.0 * width * hidden_units),
        grid=(levels, CORES),
        out_shape=(shape(master_up.shape, f32),) * 4,
        in_specs=[
            pl.BlockSpec((1, Q, 1, PARTS, deep, cols), lambda i, j: (j, 0, i, 0, 0, 0)),
            pl.BlockSpec((8, 128), lambda i, j: (0, 0)),
            flat, flat, flat, flat,
        ],
        out_specs=(flat,) * 4,
        cost_estimate=cost(8 * master_up.size, 34 * master_up.size),
        compiler_params=pltpu.CompilerParams(vmem_limit_bytes=VMEM_LIMIT),
    )(grads, squares, master_up, master_down, moment_up, moment_down)


def table_lookup(positions, table):
    onehot = (
        positions[:, None] == jnp.arange(table.shape[0], dtype=jnp.int32)[None, :]
    ).astype(jnp.bfloat16)
    return jnp.dot(onehot, table, preferred_element_type=jnp.float32)


def column_product(left, right):
    return lax.dot_general(
        left, right, (((0,), (0,)), ((), ())), preferred_element_type=jnp.float32
    )


def collective_plan(
    tokens, out_grad, segments, pos_rows, pos_cols, row_table, col_table, norm_gain,
    master_up, master_down, moment_up, moment_down,
):
    images = 8
    embedded = (
        tokens.astype(jnp.float32)
        + table_lookup(pos_rows, row_table)
        + table_lookup(pos_cols, col_table)
    )
    average = jnp.mean(embedded, axis=1, keepdims=True)
    centered = embedded - average
    variance = jnp.mean(centered * centered, axis=1, keepdims=True)
    normed = (centered * lax.rsqrt(variance + 1e-06) * norm_gain[None, :]).astype(jnp.bfloat16)
    member = (segments[0][:, None] == jnp.arange(images, dtype=jnp.int32)[None, :]).astype(
        jnp.float32
    )
    token_weight = jnp.dot(member, 1.0 / jnp.sum(member, axis=0))
    weighted = (out_grad.astype(jnp.float32) * token_weight[:, None]).astype(jnp.bfloat16)
    w_up = lax.all_gather(master_up.astype(jnp.bfloat16), "gx", axis=0, tiled=True)
    pre_act = jnp.dot(normed, w_up, preferred_element_type=jnp.float32)
    hidden, backward = jax.vjp(gelu_tanh, pre_act)
    w_down = lax.all_gather(master_down.astype(jnp.bfloat16), "gx", axis=0, tiled=True)
    hidden_grad = jnp.dot(weighted, w_down, preferred_element_type=jnp.float32)
    pre_grad = backward(hidden_grad)[0].astype(jnp.bfloat16)
    grads = [column_product(normed, pre_grad), column_product(weighted, hidden.astype(jnp.bfloat16))]
    group_sum = lax.psum_scatter(
        jnp.concatenate(grads, axis=1).astype(jnp.bfloat16), "gx", scatter_dimension=0, tiled=True
    )
    grad_sum = lax.psum(group_sum, "gy").astype(jnp.float32)
    squares = lax.psum(jnp.sum(grad_sum * grad_sum), "gx")
    entries = 2.0 * tokens.shape[1] * master_up.shape[1]
    scale = lax.rsqrt(squares / entries + 1e-06)
    half = master_up.shape[1]
    new_mu = momentum_keep * moment_up + scale * grad_sum[:, :half]
    new_md = momentum_keep * moment_down + scale * grad_sum[:, half:]
    return master_up - learn_rate * new_mu, master_down - learn_rate * new_md, new_mu, new_md


def solution(mesh):
    gx, gy = mesh.shape["gx"], mesh.shape["gy"]

    def on_device(*args):
        width, half = args[0].shape[1], args[8].shape[1] // CORES
        fits = (
            gx == 2 * CORES
            and gy % PAIR == 0
            and gy > PAIR
            and args[0].shape[0] % 128 == 0
            and width % (gx * gy // CORES * 16) == 0
            and width % (gx * 16) == 0
            and gy // PAIR % 2 == 0
            and half % (Q * 128) == 0
        )
        return (kernel_plan if fits else collective_plan)(*args)

    both, rows = P(("gx", "gy"), None), P("gx", None)
    return jax.shard_map(
        on_device,
        mesh=mesh,
        in_specs=(both, both, both, P(("gx", "gy")), P(("gx", "gy")), P(), P(), P())
        + (rows,) * 4,
        out_specs=(rows,) * 4,
        check_vma=False,
    )
```

```python
import functools

import jax
import jax.numpy as jnp
from jax import lax
from jax.experimental import pallas as pl
from jax.experimental.pallas import tpu as pltpu
from jax.sharding import PartitionSpec as P

momentum_keep = 0.9
learn_rate = 0.01
MESH = pl.DeviceIdType.MESH
VMEM = pltpu.VMEM
VMEM_LIMIT = 60 * 1024 * 1024
CORES = 2
PAIR = 2
PARTS = 2


def gelu_tanh(values):
    return (
        0.5
        * values
        * (1.0 + jnp.tanh(0.7978845608 * (values + 0.044715 * values * values * values)))
    )


def chunk_widths(columns):
    if columns % 256 or columns < 512:
        return [128] * (columns // 128)
    return [128] + [256] * (columns // 256 - 1) + [128]


class Copies:
    def __init__(self, send, recv):
        self.send, self.recv, self.count, self.all = send, recv, 0, []

    def start(self, src, dst, device):
        copy = pltpu.make_async_remote_copy(
            src_ref=src,
            dst_ref=dst,
            send_sem=self.send.at[self.count],
            recv_sem=self.recv.at[self.count],
            device_id=device,
            device_id_type=MESH,
        )
        copy.start()
        self.count += 1
        self.all.append(copy)
        return copy

    def finish(self):
        for copy in self.all:
            copy.wait_send()


def greet(devices):
    barrier = pltpu.get_barrier_semaphore()
    for device in devices:
        pl.semaphore_signal(barrier, inc=1, device_id=device, device_id_type=MESH)
    pl.semaphore_wait(barrier, len(devices))


def place():
    gx, gy = lax.axis_index("gx"), lax.axis_index("gy")
    return gx, gy, gx // CORES, lax.rem(gx, CORES), gy // PAIR, lax.rem(gy, PAIR)


def block_kernel(
    master_up, master_down, tokens, out_grad, seg, rows, cols, row_table, col_table, gain,
    out, squares,
    shard, full, normed, weighted, norm_t, weight_t, pre_grad, hidden,
    s1, r1, s2, r2, s3, r3, keep, whole, ss, ss_s, ss_r, send, recv,
):
    bf16, f32 = jnp.bfloat16, jnp.float32
    gx, gy, x, c, h, l = place()
    levels = lax.axis_size("gy") // PAIR
    partner = (x * CORES + 1 - c, gy)
    across = ((1 - x) * CORES + c, gy)
    diagonal = ((1 - x) * CORES + 1 - c, gy)
    beside = (gx, h * PAIR + 1 - l)
    odd = lax.rem(h, 2)
    neighbour = (gx, (h + 1 - 2 * odd) * PAIR + l)
    ahead = [lax.rem(h + k, levels) for k in range(levels)]
    behind = [lax.rem(h + levels - k, levels) for k in range(levels)]
    above = [(gx, ahead[k] * PAIR + l) for k in range(levels)]
    greet([partner, across, diagonal, beside] + above[1:])
    copies = Copies(send, recv)
    half = shard.shape[3]
    widths = chunk_widths(half)
    chunks = len(widths)
    at = [pl.ds(sum(widths[:q]), widths[q]) for q in range(chunks)]
    count, features = tokens.shape
    block = s1.shape[2]
    deep = block // levels

    straight, crossed, near, passed = {}, {}, {}, {}

    def send_weights(q):
        for k in range(CORES):
            start = k * half + at[q].start
            shard[k, 0, :, at[q]] = master_up[:, start : start + widths[q]].astype(bf16)
            shard[k, 1, :, at[q]] = master_down[:, start : start + widths[q]].astype(bf16)
        mine = full.at[odd, gx, :, at[q]]
        straight[q] = copies.start(shard.at[c, odd, :, at[q]], mine, across)
        crossed[q] = copies.start(shard.at[1 - c, odd, :, at[q]], mine, diagonal)
        near[q] = copies.start(
            shard.at[1 - c, :, :, at[q]], full.at[:, gx, :, at[q]], partner
        )
        for u in range(PARTS):
            full[u, gx, :, at[q]] = shard[c, u, :, at[q]]

    def pass_weights(q):
        for k, (arrived, owner) in enumerate(((straight[q], across[0]), (crossed[q], diagonal[0]))):
            arrived.wait_recv()
            piece = full.at[odd, owner, :, at[q]]
            passed[q, k] = copies.start(piece, piece, neighbour)

    def column(row, lanes):
        return jnp.broadcast_to(row, (lanes, row.shape[1])).T

    def layer_norm():
        grid, tile = row_table.shape[0], 128
        images = lax.broadcasted_iota(jnp.int32, (128, count), 0)
        member = (jnp.broadcast_to(seg[...], (128, count)) == images).astype(f32)
        sizes = jnp.maximum(jnp.sum(member, axis=1, keepdims=True), 1.0)
        token_weight = jnp.sum(member * (1.0 / sizes), axis=0, keepdims=True)
        places = lax.broadcasted_iota(jnp.int32, (tile, 128), 1)
        for i in range(count // tile):
            span = slice(i * tile, (i + 1) * tile)
            own = pl.ds(pl.multiple_of(c * count + i * tile, tile), tile)
            embedded = tokens[span, :].astype(f32)
            for index, table in ((rows, row_table), (cols, col_table)):
                hot = column(index[:, span].astype(f32), 128)[:, :grid] == places[:, :grid].astype(f32)
                embedded += jnp.dot(
                    hot.astype(f32).astype(bf16), table[...], preferred_element_type=f32
                )
            average = jnp.mean(embedded, axis=1, keepdims=True)
            centered = embedded - average
            variance = jnp.mean(centered * centered, axis=1, keepdims=True)
            left = (centered * lax.rsqrt(variance + 1e-06) * gain[...]).astype(bf16)
            normed[own, :] = left
            norm_t[c, :, span] = left.T
            weight = column(token_weight[:, span], 128)[:, :1]
            right = (out_grad[span, :].astype(f32) * weight).astype(bf16)
            weighted[own, :] = right
            weight_t[c, :, span] = right.T

    def forward(q):
        near[q].wait_recv()
        for k in range(2):
            passed[q, k].wait_recv()
        tile = 256
        width = widths[q]
        total = CORES * count

        @pl.loop(0, total // tile)
        def _(i):
            own = pl.ds(pl.multiple_of(i * tile, tile), tile)
            v = jnp.dot(
                normed[own, :], full[0, :, :, at[q]].reshape(features, width), preferred_element_type=f32
            )
            grad = jnp.dot(
                weighted[own, :], full[1, :, :, at[q]].reshape(features, width), preferred_element_type=f32
            )
            square = v * v
            t = jnp.tanh(0.7978845608 * (v + 0.044715 * (square * v)))
            rising = 0.5 * (1.0 + t)
            slope = 0.7978845608 * (1.0 + 3.0 * 0.044715 * square)
            hidden[own, at[q]] = (v * rising).astype(bf16)
            pre_grad[own, at[q]] = (grad * (rising + 0.5 * v * (1.0 - t * t) * slope)).astype(bf16)

    def product(p, q, at_x, at_l):
        own = pl.ds(pl.multiple_of((at_x * PAIR + at_l) * block, 16), block)
        left, right = ((norm_t, pre_grad), (weight_t, hidden))[p]
        return sum(
            jnp.dot(
                left[k, own, :],
                right[k * count : (k + 1) * count, at[q]],
                preferred_element_type=f32,
            )
            for k in range(CORES)
        )

    first, second, third, spread, beyond, last = {}, {}, {}, {}, {}, {}
    targets = (across, beside)

    def send_first(q):
        for slot in range(2):
            for p in range(PARTS):
                where = (1 - x, 1 - l) if slot == 0 else ((1 - x, l), (x, 1 - l))[p]
                s1[p, slot, :, at[q]] = product(p, q, *where).astype(bf16)
                first[q, p, slot] = copies.start(
                    s1.at[p, slot, :, at[q]], r1.at[p, slot, :, at[q]], targets[p]
                )

    def send_second(q):
        for p in range(PARTS):
            own = product(p, q, *((x, 1 - l), (1 - x, l))[p])
            first[q, p, 0].wait_recv()
            s2[p, :, at[q]] = (own + r1[p, 0, :, at[q]].astype(f32)).astype(bf16)
            second[q, p] = copies.start(s2.at[p, :, at[q]], r2.at[p, :, at[q]], targets[1 - p])

    def send_third(q):
        for p in range(PARTS):
            own = product(p, q, x, l)
            first[q, p, 1].wait_recv()
            second[q, p].wait_recv()
            total = own + r1[p, 1, :, at[q]].astype(f32) + r2[p, :, at[q]].astype(f32)
            for level in range(levels):
                piece = total[level * deep : (level + 1) * deep]
                keep[level, p, :, at[q]] = piece
                s3[level, p, :, at[q]] = piece.astype(bf16)
        for k in range(1, levels):
            third[q, k] = copies.start(
                s3.at[ahead[k], :, :, at[q]], r3.at[h, :, :, at[q]], above[k]
            )

    def send_whole(q):
        for k in range(1, levels):
            third[q, k].wait_recv()
        for p in range(PARTS):
            total = keep[h, p, :, at[q]]
            for k in range(1, levels):
                total = total + r3[behind[k], p, :, at[q]].astype(f32)
            whole[l, h, p, :, at[q]] = total.astype(bf16)
            power = jnp.sum((total * total).reshape(deep // 8, 8, widths[q]), axis=0)
            for lane in range(widths[q] // 128):
                ss[...] += power[:, lane * 128 : (lane + 1) * 128]
        piece = whole.at[l, h, :, :, at[q]]
        for k in range(1, levels):
            spread[q, k] = copies.start(piece, piece, above[k])
        beyond[q, 0] = copies.start(piece, piece, beside)

    def pass_whole(q):
        for k in range(1, levels):
            spread[q, k].wait_recv()
            piece = whole.at[l, behind[k], :, :, at[q]]
            beyond[q, k] = copies.start(piece, piece, beside)

    def send_last(q):
        for k in range(levels):
            beyond[q, k].wait_recv()
        last[q] = copies.start(
            whole.at[1 - c, :, :, :, at[q]], out.at[c, :, :, :, at[q]], partner
        )
        out[c, :, :, :, at[q]] = whole[c, :, :, :, at[q]]

    def add_squares():
        ss_s[0] = ss[...]
        waits = [copies.start(ss_s.at[0], ss_r.at[h], above[k]) for k in range(1, levels)]
        ss_r[h] = ss[...]
        for copy in waits:
            copy.wait_recv()
        running = ss_r[0]
        for level in range(1, levels):
            running = running + ss_r[level]
        for turn, target in enumerate((beside, across, partner)):
            ss_s[1 + turn] = running
            copies.start(ss_s.at[1 + turn], ss_r.at[levels + turn], target).wait_recv()
            running = running + ss_r[levels + turn]
        squares[...] = running

    ss[...] = jnp.zeros_like(ss)
    send_weights(0)
    layer_norm()
    mine = pl.ds(pl.multiple_of(c * count, 128), count)
    shared = [
        copies.start(piece, piece, partner)
        for piece in (normed.at[mine], weighted.at[mine], norm_t.at[c], weight_t.at[c])
    ]
    pass_weights(0)
    send_weights(1)
    for copy in shared:
        copy.wait_recv()
    order = (
        (0, forward), (5, send_last), (4, pass_whole), (3, send_whole),
        (2, send_third), (1, send_second), (0, send_first),
    )
    for tick in range(chunks + 5):
        if 0 < tick and tick + 1 < chunks:
            send_weights(tick + 1)
        for lag, action in order:
            if 0 <= tick - lag < chunks:
                action(tick - lag)
            if lag == 0 and action is forward and tick + 1 < chunks:
                pass_weights(tick + 1)
        if tick == chunks + 2:
            add_squares()
    for q in range(chunks):
        last[q].wait_recv()
    copies.finish()


def update_kernel(
    entries, grads, squares, up, down, moment_up, moment_down, new_up, new_down, new_mu, new_md
):
    scale = lax.rsqrt(jnp.sum(squares[...]) / entries + 1e-06)
    for p, old, moment, new, new_moment in (
        (0, up, moment_up, new_up, new_mu),
        (1, down, moment_down, new_down, new_md),
    ):
        fresh = momentum_keep * moment[...] + scale * grads[0, 0, p].astype(jnp.float32)
        new_moment[...] = fresh
        new[...] = old[...] - learn_rate * fresh


def cost(flops, moved):
    return pl.CostEstimate(flops=flops, bytes_accessed=moved, transcendentals=0)


def kernel_plan(
    tokens, out_grad, segments, pos_rows, pos_cols, row_table, col_table, norm_gain,
    master_up, master_down, moment_up, moment_down,
):
    bf16, f32 = jnp.bfloat16, jnp.float32
    shape = jax.ShapeDtypeStruct
    count, width = tokens.shape
    depth, hidden_units = master_up.shape
    gx, gy = lax.axis_size("gx"), lax.axis_size("gy")
    levels = gy // PAIR
    half = hidden_units // CORES
    both = CORES * count
    block = width // (gx // CORES) // PAIR
    deep = block // levels
    chunks = len(chunk_widths(half))
    vm = pl.BlockSpec(memory_space=VMEM)
    n_copies = chunks * (11 + 2 * (levels - 1) + levels + 1) + 4 + levels + 2
    grads, squares = pl.pallas_call(
        block_kernel,
        out_shape=(shape((CORES, levels, PARTS, deep, half), bf16), shape((8, 128), f32)),
        in_specs=[vm] * 10,
        out_specs=(vm, vm),
        scratch_shapes=[
            VMEM((CORES, PARTS, depth, half), bf16),
            VMEM((PARTS, gx, depth, half), bf16),
            VMEM((both, width), bf16),
            VMEM((both, width), bf16),
            VMEM((CORES, width, count), bf16),
            VMEM((CORES, width, count), bf16),
            VMEM((both, half), bf16),
            VMEM((both, half), bf16),
            VMEM((PARTS, 2, block, half), bf16),
            VMEM((PARTS, 2, block, half), bf16),
            VMEM((PARTS, block, half), bf16),
            VMEM((PARTS, block, half), bf16),
            VMEM((levels, PARTS, deep, half), bf16),
            VMEM((levels, PARTS, deep, half), bf16),
            VMEM((levels, PARTS, deep, half), f32),
            VMEM((PAIR, levels, PARTS, deep, half), bf16),
            VMEM((8, 128), f32),
            VMEM((4, 8, 128), f32),
            VMEM((levels + 3, 8, 128), f32),
            pltpu.SemaphoreType.DMA((n_copies,)),
            pltpu.SemaphoreType.DMA((n_copies,)),
        ],
        cost_estimate=cost(8 * both * width * half, 8 * both * width),
        compiler_params=pltpu.CompilerParams(
            collective_id=0, has_side_effects=True, vmem_limit_bytes=VMEM_LIMIT
        ),
    )(
        master_up,
        master_down,
        tokens,
        out_grad,
        segments,
        pos_rows.reshape(1, count),
        pos_cols.reshape(1, count),
        row_table,
        col_table,
        norm_gain.reshape(1, width),
    )

    flat = pl.BlockSpec((deep, half), lambda i, j: (i, j))
    return pl.pallas_call(
        functools.partial(update_kernel, 2.0 * width * hidden_units),
        grid=(levels, CORES),
        out_shape=(shape(master_up.shape, f32),) * 4,
        in_specs=[
            pl.BlockSpec((1, 1, PARTS, deep, half), lambda i, j: (j, i, 0, 0, 0)),
            pl.BlockSpec((8, 128), lambda i, j: (0, 0)),
            flat, flat, flat, flat,
        ],
        out_specs=(flat,) * 4,
        cost_estimate=cost(8 * master_up.size, 34 * master_up.size),
        compiler_params=pltpu.CompilerParams(vmem_limit_bytes=VMEM_LIMIT),
    )(grads, squares, master_up, master_down, moment_up, moment_down)


def table_lookup(positions, table):
    onehot = (
        positions[:, None] == jnp.arange(table.shape[0], dtype=jnp.int32)[None, :]
    ).astype(jnp.bfloat16)
    return jnp.dot(onehot, table, preferred_element_type=jnp.float32)


def column_product(left, right):
    return lax.dot_general(
        left, right, (((0,), (0,)), ((), ())), preferred_element_type=jnp.float32
    )


def collective_plan(
    tokens, out_grad, segments, pos_rows, pos_cols, row_table, col_table, norm_gain,
    master_up, master_down, moment_up, moment_down,
):
    images = 8
    embedded = (
        tokens.astype(jnp.float32)
        + table_lookup(pos_rows, row_table)
        + table_lookup(pos_cols, col_table)
    )
    average = jnp.mean(embedded, axis=1, keepdims=True)
    centered = embedded - average
    variance = jnp.mean(centered * centered, axis=1, keepdims=True)
    normed = (centered * lax.rsqrt(variance + 1e-06) * norm_gain[None, :]).astype(jnp.bfloat16)
    member = (segments[0][:, None] == jnp.arange(images, dtype=jnp.int32)[None, :]).astype(
        jnp.float32
    )
    token_weight = jnp.dot(member, 1.0 / jnp.sum(member, axis=0))
    weighted = (out_grad.astype(jnp.float32) * token_weight[:, None]).astype(jnp.bfloat16)
    w_up = lax.all_gather(master_up.astype(jnp.bfloat16), "gx", axis=0, tiled=True)
    pre_act = jnp.dot(normed, w_up, preferred_element_type=jnp.float32)
    hidden, backward = jax.vjp(gelu_tanh, pre_act)
    w_down = lax.all_gather(master_down.astype(jnp.bfloat16), "gx", axis=0, tiled=True)
    hidden_grad = jnp.dot(weighted, w_down, preferred_element_type=jnp.float32)
    pre_grad = backward(hidden_grad)[0].astype(jnp.bfloat16)
    grads = [column_product(normed, pre_grad), column_product(weighted, hidden.astype(jnp.bfloat16))]
    group_sum = lax.psum_scatter(
        jnp.concatenate(grads, axis=1).astype(jnp.bfloat16), "gx", scatter_dimension=0, tiled=True
    )
    grad_sum = lax.psum(group_sum, "gy").astype(jnp.float32)
    squares = lax.psum(jnp.sum(grad_sum * grad_sum), "gx")
    entries = 2.0 * tokens.shape[1] * master_up.shape[1]
    scale = lax.rsqrt(squares / entries + 1e-06)
    half = master_up.shape[1]
    new_mu = momentum_keep * moment_up + scale * grad_sum[:, :half]
    new_md = momentum_keep * moment_down + scale * grad_sum[:, half:]
    return master_up - learn_rate * new_mu, master_down - learn_rate * new_md, new_mu, new_md


def solution(mesh):
    gx, gy = mesh.shape["gx"], mesh.shape["gy"]

    def on_device(*args):
        width, half = args[0].shape[1], args[8].shape[1] // CORES
        fits = (
            gx == 2 * CORES
            and gy % PAIR == 0
            and gy > PAIR
            and args[0].shape[0] % 128 == 0
            and width % (gx * gy // CORES * 16) == 0
            and width % (gx * 16) == 0
            and gy // PAIR % 2 == 0
            and half % 128 == 0
        )
        return (kernel_plan if fits else collective_plan)(*args)

    both, rows = P(("gx", "gy"), None), P("gx", None)
    return jax.shard_map(
        on_device,
        mesh=mesh,
        in_specs=(both, both, both, P(("gx", "gy")), P(("gx", "gy")), P(), P(), P())
        + (rows,) * 4,
        out_specs=(rows,) * 4,
        check_vma=False,
    )
```

```python
import functools

import jax
import jax.numpy as jnp
from jax import lax
from jax.experimental import pallas as pl
from jax.experimental.pallas import tpu as pltpu
from jax.sharding import PartitionSpec as P

momentum_keep = 0.9
learn_rate = 0.01
MESH = pl.DeviceIdType.MESH
VMEM = pltpu.VMEM
VMEM_LIMIT = 60 * 1024 * 1024
CORES = 2
PAIR = 2
PARTS = 2


def gelu_tanh(values):
    return (
        0.5
        * values
        * (1.0 + jnp.tanh(0.7978845608 * (values + 0.044715 * values * values * values)))
    )


def chunk_widths(columns):
    if columns % 256 or columns < 512:
        return [128] * (columns // 128)
    return [128] + [256] * (columns // 256 - 1) + [128]


class Copies:
    def __init__(self, send, recv):
        self.send, self.recv, self.count, self.all = send, recv, 0, []

    def start(self, src, dst, device):
        copy = pltpu.make_async_remote_copy(
            src_ref=src,
            dst_ref=dst,
            send_sem=self.send.at[self.count],
            recv_sem=self.recv.at[self.count],
            device_id=device,
            device_id_type=MESH,
        )
        copy.start()
        self.count += 1
        self.all.append(copy)
        return copy

    def finish(self):
        for copy in self.all:
            copy.wait_send()


def greet(devices):
    barrier = pltpu.get_barrier_semaphore()
    for device in devices:
        pl.semaphore_signal(barrier, inc=1, device_id=device, device_id_type=MESH)
    pl.semaphore_wait(barrier, len(devices))


def place():
    gx, gy = lax.axis_index("gx"), lax.axis_index("gy")
    return gx, gy, gx // CORES, lax.rem(gx, CORES), gy // PAIR, lax.rem(gy, PAIR)


def block_kernel(
    master_up, master_down, tokens, out_grad, seg, rows, cols, row_table, col_table, gain,
    out, squares,
    shard, full, normed, weighted, norm_t, weight_t, pre_grad, hidden,
    s1, r1, s2, r2, s3, r3, keep, whole, ss, ss_s, ss_r, send, recv,
):
    bf16, f32 = jnp.bfloat16, jnp.float32
    gx, gy, x, c, h, l = place()
    levels = lax.axis_size("gy") // PAIR
    partner = (x * CORES + 1 - c, gy)
    across = ((1 - x) * CORES + c, gy)
    diagonal = ((1 - x) * CORES + 1 - c, gy)
    beside = (gx, h * PAIR + 1 - l)
    odd = lax.rem(h, 2)
    neighbour = (gx, (h + 1 - 2 * odd) * PAIR + l)
    ahead = [lax.rem(h + k, levels) for k in range(levels)]
    behind = [lax.rem(h + levels - k, levels) for k in range(levels)]
    above = [(gx, ahead[k] * PAIR + l) for k in range(levels)]
    greet([partner, across, diagonal, beside] + above[1:])
    copies = Copies(send, recv)
    half = master_up.shape[1] // CORES
    widths = [piece.shape[3] for piece in shard]
    chunks = len(widths)
    offset = [sum(widths[:q]) for q in range(chunks)]
    count, features = tokens.shape
    block = s1[0].shape[2]
    deep = block // levels

    straight, crossed, near, passed = {}, {}, {}, {}

    def send_weights(q):
        for k in range(CORES):
            start = k * half + offset[q]
            shard[q][k, 0, :, :] = master_up[:, start : start + widths[q]].astype(bf16)
            shard[q][k, 1, :, :] = master_down[:, start : start + widths[q]].astype(bf16)
        mine = full[q].at[odd, gx]
        straight[q] = copies.start(shard[q].at[c, odd], mine, across)
        crossed[q] = copies.start(shard[q].at[1 - c, odd], mine, diagonal)
        near[q] = copies.start(
            shard[q].at[1 - c], full[q].at[:, gx], partner
        )
        for u in range(PARTS):
            full[q][u, gx, :, :] = shard[q][c, u, :, :]

    def pass_weights(q):
        for k, (arrived, owner) in enumerate(((straight[q], across[0]), (crossed[q], diagonal[0]))):
            arrived.wait_recv()
            piece = full[q].at[odd, owner]
            passed[q, k] = copies.start(piece, piece, neighbour)

    def column(row, lanes):
        return jnp.broadcast_to(row, (lanes, row.shape[1])).T

    def layer_norm():
        grid, tile = row_table.shape[0], 128
        images = lax.broadcasted_iota(jnp.int32, (128, count), 0)
        member = (jnp.broadcast_to(seg[...], (128, count)) == images).astype(f32)
        sizes = jnp.maximum(jnp.sum(member, axis=1, keepdims=True), 1.0)
        token_weight = jnp.sum(member * (1.0 / sizes), axis=0, keepdims=True)
        places = lax.broadcasted_iota(jnp.int32, (tile, 128), 1)
        for i in range(count // tile):
            span = slice(i * tile, (i + 1) * tile)
            own = pl.ds(pl.multiple_of(c * count + i * tile, tile), tile)
            embedded = tokens[span, :].astype(f32)
            for index, table in ((rows, row_table), (cols, col_table)):
                hot = column(index[:, span].astype(f32), 128)[:, :grid] == places[:, :grid].astype(f32)
                embedded += jnp.dot(
                    hot.astype(f32).astype(bf16), table[...], preferred_element_type=f32
                )
            average = jnp.mean(embedded, axis=1, keepdims=True)
            centered = embedded - average
            variance = jnp.mean(centered * centered, axis=1, keepdims=True)
            left = (centered * lax.rsqrt(variance + 1e-06) * gain[...]).astype(bf16)
            normed[own, :] = left
            norm_t[c, :, span] = left.T
            weight = column(token_weight[:, span], 128)[:, :1]
            right = (out_grad[span, :].astype(f32) * weight).astype(bf16)
            weighted[own, :] = right
            weight_t[c, :, span] = right.T

    def forward(q):
        near[q].wait_recv()
        for k in range(2):
            passed[q, k].wait_recv()
        tile = 256
        width = widths[q]
        total = CORES * count

        @pl.loop(0, total // tile)
        def _(i):
            own = pl.ds(pl.multiple_of(i * tile, tile), tile)
            v = jnp.dot(
                normed[own, :], full[q][0, :, :, :].reshape(features, width), preferred_element_type=f32
            )
            grad = jnp.dot(
                weighted[own, :], full[q][1, :, :, :].reshape(features, width), preferred_element_type=f32
            )
            square = v * v
            t = jnp.tanh(0.7978845608 * (v + 0.044715 * (square * v)))
            rising = 0.5 * (1.0 + t)
            slope = 0.7978845608 * (1.0 + 3.0 * 0.044715 * square)
            hidden[q][own, :] = (v * rising).astype(bf16)
            pre_grad[q][own, :] = (grad * (rising + 0.5 * v * (1.0 - t * t) * slope)).astype(bf16)

    def product(p, q, at_x, at_l):
        own = pl.ds(pl.multiple_of((at_x * PAIR + at_l) * block, 16), block)
        left, right = ((norm_t, pre_grad), (weight_t, hidden))[p]
        return sum(
            jnp.dot(
                left[k, own, :],
                right[q][k * count : (k + 1) * count, :],
                preferred_element_type=f32,
            )
            for k in range(CORES)
        )

    first, second, third, spread, beyond, last = {}, {}, {}, {}, {}, {}
    targets = (across, beside)

    def send_first(q):
        for slot in range(2):
            for p in range(PARTS):
                where = (1 - x, 1 - l) if slot == 0 else ((1 - x, l), (x, 1 - l))[p]
                s1[q][p, slot, :, :] = product(p, q, *where).astype(bf16)
                first[q, p, slot] = copies.start(
                    s1[q].at[p, slot], r1[q].at[p, slot], targets[p]
                )

    def send_second(q):
        for p in range(PARTS):
            own = product(p, q, *((x, 1 - l), (1 - x, l))[p])
            first[q, p, 0].wait_recv()
            s2[q][p, :, :] = (own + r1[q][p, 0, :, :].astype(f32)).astype(bf16)
            second[q, p] = copies.start(s2[q].at[p], r2[q].at[p], targets[1 - p])

    def send_third(q):
        for p in range(PARTS):
            own = product(p, q, x, l)
            first[q, p, 1].wait_recv()
            second[q, p].wait_recv()
            total = own + r1[q][p, 1, :, :].astype(f32) + r2[q][p, :, :].astype(f32)
            for level in range(levels):
                piece = total[level * deep : (level + 1) * deep]
                keep[q][level, p, :, :] = piece
                s3[q][level, p, :, :] = piece.astype(bf16)
        for k in range(1, levels):
            third[q, k] = copies.start(
                s3[q].at[ahead[k]], r3[q].at[h], above[k]
            )

    def send_whole(q):
        for k in range(1, levels):
            third[q, k].wait_recv()
        for p in range(PARTS):
            total = keep[q][h, p, :, :]
            for k in range(1, levels):
                total = total + r3[q][behind[k], p, :, :].astype(f32)
            whole[q][l, h, p, :, :] = total.astype(bf16)
            power = jnp.sum((total * total).reshape(deep // 8, 8, widths[q]), axis=0)
            for lane in range(widths[q] // 128):
                ss[...] += power[:, lane * 128 : (lane + 1) * 128]
        piece = whole[q].at[l, h]
        for k in range(1, levels):
            spread[q, k] = copies.start(piece, piece, above[k])
        beyond[q, 0] = copies.start(piece, piece, beside)

    def pass_whole(q):
        for k in range(1, levels):
            spread[q, k].wait_recv()
            piece = whole[q].at[l, behind[k]]
            beyond[q, k] = copies.start(piece, piece, beside)

    def send_last(q):
        for k in range(levels):
            beyond[q, k].wait_recv()
        last[q] = copies.start(
            whole[q].at[1 - c], out[q].at[c], partner
        )
        out[q][c, :, :, :, :] = whole[q][c, :, :, :, :]

    def add_squares():
        ss_s[0] = ss[...]
        waits = [copies.start(ss_s.at[0], ss_r.at[h], above[k]) for k in range(1, levels)]
        ss_r[h] = ss[...]
        yield
        for copy in waits:
            copy.wait_recv()
        running = ss_r[0]
        for level in range(1, levels):
            running = running + ss_r[level]
        for turn, target in enumerate((beside, across, partner)):
            ss_s[1 + turn] = running
            copy = copies.start(ss_s.at[1 + turn], ss_r.at[levels + turn], target)
            yield
            copy.wait_recv()
            running = running + ss_r[levels + turn]
        squares[...] = running

    ss[...] = jnp.zeros_like(ss)
    send_weights(0)
    send_weights(1)
    layer_norm()
    mine = pl.ds(pl.multiple_of(c * count, 128), count)
    shared = [
        copies.start(piece, piece, partner)
        for piece in (normed.at[mine], weighted.at[mine], norm_t.at[c], weight_t.at[c])
    ]
    pass_weights(0)
    for copy in shared:
        copy.wait_recv()
    stages = forward, send_first, send_second, send_third, send_whole, pass_whole, send_last
    turns = add_squares()
    for tick in range(chunks + 5):
        if tick + 2 < chunks:
            send_weights(tick + 2)
        if tick + 1 < chunks:
            pass_weights(tick + 1)
        for stage, action in enumerate(stages):
            lag = max(stage - 1, 0)
            if 0 <= tick - lag < chunks:
                action(tick - lag)
        if tick >= chunks + 2:
            next(turns)
    for _ in turns:
        pass
    for q in range(chunks):
        last[q].wait_recv()
    copies.finish()


def update_kernel(
    entries, grads, squares, up, down, moment_up, moment_down, new_up, new_down, new_mu, new_md
):
    scale = lax.rsqrt(jnp.sum(squares[...]) / entries + 1e-06)
    end = 0
    for grad in grads:
        start, end = end, end + grad.shape[4]
        for p, old, moment, new, new_moment in (
            (0, up, moment_up, new_up, new_mu),
            (1, down, moment_down, new_down, new_md),
        ):
            fresh = momentum_keep * moment[:, start:end] + scale * grad[0, 0, p].astype(jnp.float32)
            new_moment[:, start:end] = fresh
            new[:, start:end] = old[:, start:end] - learn_rate * fresh


def cost(flops, moved):
    return pl.CostEstimate(flops=flops, bytes_accessed=moved, transcendentals=0)


def kernel_plan(
    tokens, out_grad, segments, pos_rows, pos_cols, row_table, col_table, norm_gain,
    master_up, master_down, moment_up, moment_down,
):
    bf16, f32 = jnp.bfloat16, jnp.float32
    shape = jax.ShapeDtypeStruct
    count, width = tokens.shape
    depth, hidden_units = master_up.shape
    gx, gy = lax.axis_size("gx"), lax.axis_size("gy")
    levels = gy // PAIR
    half = hidden_units // CORES
    both = CORES * count
    block = width // (gx // CORES) // PAIR
    deep = block // levels
    widths = chunk_widths(half)
    chunks = len(widths)

    def split(*lead):
        return [VMEM(lead + (w,), bf16) for w in widths]

    vm = pl.BlockSpec(memory_space=VMEM)
    n_copies = chunks * (11 + 2 * (levels - 1) + levels + 1) + 4 + levels + 2
    grads, squares = pl.pallas_call(
        block_kernel,
        out_shape=(
            [shape((CORES, levels, PARTS, deep, w), bf16) for w in widths],
            shape((8, 128), f32),
        ),
        in_specs=[vm] * 10,
        out_specs=([vm] * chunks, vm),
        scratch_shapes=[
            split(CORES, PARTS, depth),
            split(PARTS, gx, depth),
            VMEM((both, width), bf16),
            VMEM((both, width), bf16),
            VMEM((CORES, width, count), bf16),
            VMEM((CORES, width, count), bf16),
            split(both),
            split(both),
            split(PARTS, 2, block),
            split(PARTS, 2, block),
            split(PARTS, block),
            split(PARTS, block),
            split(levels, PARTS, deep),
            split(levels, PARTS, deep),
            [VMEM((levels, PARTS, deep, w), f32) for w in widths],
            split(PAIR, levels, PARTS, deep),
            VMEM((8, 128), f32),
            VMEM((4, 8, 128), f32),
            VMEM((levels + 3, 8, 128), f32),
            pltpu.SemaphoreType.DMA((n_copies,)),
            pltpu.SemaphoreType.DMA((n_copies,)),
        ],
        cost_estimate=cost(8 * both * width * half, 8 * both * width),
        compiler_params=pltpu.CompilerParams(
            collective_id=0, has_side_effects=True, vmem_limit_bytes=VMEM_LIMIT
        ),
    )(
        master_up,
        master_down,
        tokens,
        out_grad,
        segments,
        pos_rows.reshape(1, count),
        pos_cols.reshape(1, count),
        row_table,
        col_table,
        norm_gain.reshape(1, width),
    )

    flat = pl.BlockSpec((deep, half), lambda i, j: (i, j))
    return pl.pallas_call(
        functools.partial(update_kernel, 2.0 * width * hidden_units),
        grid=(levels, CORES),
        out_shape=(shape(master_up.shape, f32),) * 4,
        in_specs=[
            [
                pl.BlockSpec((1, 1, PARTS, deep, w), lambda i, j: (j, i, 0, 0, 0))
                for w in widths
            ],
            pl.BlockSpec((8, 128), lambda i, j: (0, 0)),
            flat, flat, flat, flat,
        ],
        out_specs=(flat,) * 4,
        cost_estimate=cost(8 * master_up.size, 34 * master_up.size),
        compiler_params=pltpu.CompilerParams(vmem_limit_bytes=VMEM_LIMIT),
    )(grads, squares, master_up, master_down, moment_up, moment_down)


def table_lookup(positions, table):
    onehot = (
        positions[:, None] == jnp.arange(table.shape[0], dtype=jnp.int32)[None, :]
    ).astype(jnp.bfloat16)
    return jnp.dot(onehot, table, preferred_element_type=jnp.float32)


def column_product(left, right):
    return lax.dot_general(
        left, right, (((0,), (0,)), ((), ())), preferred_element_type=jnp.float32
    )


def collective_plan(
    tokens, out_grad, segments, pos_rows, pos_cols, row_table, col_table, norm_gain,
    master_up, master_down, moment_up, moment_down,
):
    images = 8
    embedded = (
        tokens.astype(jnp.float32)
        + table_lookup(pos_rows, row_table)
        + table_lookup(pos_cols, col_table)
    )
    average = jnp.mean(embedded, axis=1, keepdims=True)
    centered = embedded - average
    variance = jnp.mean(centered * centered, axis=1, keepdims=True)
    normed = (centered * lax.rsqrt(variance + 1e-06) * norm_gain[None, :]).astype(jnp.bfloat16)
    member = (segments[0][:, None] == jnp.arange(images, dtype=jnp.int32)[None, :]).astype(
        jnp.float32
    )
    token_weight = jnp.dot(member, 1.0 / jnp.sum(member, axis=0))
    weighted = (out_grad.astype(jnp.float32) * token_weight[:, None]).astype(jnp.bfloat16)
    w_up = lax.all_gather(master_up.astype(jnp.bfloat16), "gx", axis=0, tiled=True)
    pre_act = jnp.dot(normed, w_up, preferred_element_type=jnp.float32)
    hidden, backward = jax.vjp(gelu_tanh, pre_act)
    w_down = lax.all_gather(master_down.astype(jnp.bfloat16), "gx", axis=0, tiled=True)
    hidden_grad = jnp.dot(weighted, w_down, preferred_element_type=jnp.float32)
    pre_grad = backward(hidden_grad)[0].astype(jnp.bfloat16)
    grads = [column_product(normed, pre_grad), column_product(weighted, hidden.astype(jnp.bfloat16))]
    group_sum = lax.psum_scatter(
        jnp.concatenate(grads, axis=1).astype(jnp.bfloat16), "gx", scatter_dimension=0, tiled=True
    )
    grad_sum = lax.psum(group_sum, "gy").astype(jnp.float32)
    squares = lax.psum(jnp.sum(grad_sum * grad_sum), "gx")
    entries = 2.0 * tokens.shape[1] * master_up.shape[1]
    scale = lax.rsqrt(squares / entries + 1e-06)
    half = master_up.shape[1]
    new_mu = momentum_keep * moment_up + scale * grad_sum[:, :half]
    new_md = momentum_keep * moment_down + scale * grad_sum[:, half:]
    return master_up - learn_rate * new_mu, master_down - learn_rate * new_md, new_mu, new_md


def solution(mesh):
    gx, gy = mesh.shape["gx"], mesh.shape["gy"]

    def on_device(*args):
        width, half = args[0].shape[1], args[8].shape[1] // CORES
        fits = (
            gx == 2 * CORES
            and gy % PAIR == 0
            and gy > PAIR
            and args[0].shape[0] % 128 == 0
            and width % (gx * gy // CORES * 16) == 0
            and width % (gx * 16) == 0
            and gy // PAIR % 2 == 0
            and half % 128 == 0
        )
        return (kernel_plan if fits else collective_plan)(*args)

    both, rows = P(("gx", "gy"), None), P("gx", None)
    return jax.shard_map(
        on_device,
        mesh=mesh,
        in_specs=(both, both, both, P(("gx", "gy")), P(("gx", "gy")), P(), P(), P())
        + (rows,) * 4,
        out_specs=(rows,) * 4,
        check_vma=False,
    )
```

```python
import functools

import jax
import jax.numpy as jnp
from jax import lax
from jax.experimental import pallas as pl
from jax.experimental.pallas import tpu as pltpu
from jax.sharding import PartitionSpec as P

momentum_keep = 0.9
learn_rate = 0.01
MESH = pl.DeviceIdType.MESH
VMEM = pltpu.VMEM
VMEM_LIMIT = 60 * 1024 * 1024
CORES = 2
PAIR = 2
PARTS = 2


def gelu_tanh(values):
    return (
        0.5
        * values
        * (1.0 + jnp.tanh(0.7978845608 * (values + 0.044715 * values * values * values)))
    )


def chunk_widths(columns):
    if columns % 256 or columns < 768:
        return [128] * (columns // 128)
    return [128] * 2 + [256] * (columns // 256 - 2) + [128] * 2


class Copies:
    def __init__(self, send, recv):
        self.send, self.recv, self.count, self.all = send, recv, 0, []

    def start(self, src, dst, device):
        copy = pltpu.make_async_remote_copy(
            src_ref=src,
            dst_ref=dst,
            send_sem=self.send.at[self.count],
            recv_sem=self.recv.at[self.count],
            device_id=device,
            device_id_type=MESH,
        )
        copy.start()
        self.count += 1
        self.all.append(copy)
        return copy

    def finish(self):
        for copy in self.all:
            copy.wait_send()


def greet(devices):
    barrier = pltpu.get_barrier_semaphore()
    for device in devices:
        pl.semaphore_signal(barrier, inc=1, device_id=device, device_id_type=MESH)
    pl.semaphore_wait(barrier, len(devices))


def place():
    gx, gy = lax.axis_index("gx"), lax.axis_index("gy")
    return gx, gy, gx // CORES, lax.rem(gx, CORES), gy // PAIR, lax.rem(gy, PAIR)


def block_kernel(
    master_up, master_down, tokens, out_grad, seg, rows, cols, row_table, col_table, gain,
    out, squares,
    shard, full, normed, weighted, norm_t, weight_t, pre_grad, hidden,
    s1, r1, s2, r2, s3, r3, keep, whole, ss, ss_s, ss_r, send, recv,
):
    bf16, f32 = jnp.bfloat16, jnp.float32
    gx, gy, x, c, h, l = place()
    levels = lax.axis_size("gy") // PAIR
    partner = (x * CORES + 1 - c, gy)
    across = ((1 - x) * CORES + c, gy)
    diagonal = ((1 - x) * CORES + 1 - c, gy)
    beside = (gx, h * PAIR + 1 - l)
    odd = lax.rem(h, 2)
    neighbour = (gx, (h + 1 - 2 * odd) * PAIR + l)
    ahead = [lax.rem(h + k, levels) for k in range(levels)]
    behind = [lax.rem(h + levels - k, levels) for k in range(levels)]
    above = [(gx, ahead[k] * PAIR + l) for k in range(levels)]
    greet([partner, across, diagonal, beside] + above[1:])
    copies = Copies(send, recv)
    half = master_up.shape[1] // CORES
    widths = [piece.shape[3] for piece in shard]
    chunks = len(widths)
    offset = [sum(widths[:q]) for q in range(chunks)]
    count, features = tokens.shape
    block = s1[0].shape[2]
    deep = block // levels

    straight, crossed, near, passed = {}, {}, {}, {}

    def send_weights(q):
        for k in range(CORES):
            start = k * half + offset[q]
            shard[q][k, 0, :, :] = master_up[:, start : start + widths[q]].astype(bf16)
            shard[q][k, 1, :, :] = master_down[:, start : start + widths[q]].astype(bf16)
        mine = full[q].at[odd, gx]
        straight[q] = copies.start(shard[q].at[c, odd], mine, across)
        crossed[q] = copies.start(shard[q].at[1 - c, odd], mine, diagonal)
        near[q] = copies.start(
            shard[q].at[1 - c], full[q].at[:, gx], partner
        )
        for u in range(PARTS):
            full[q][u, gx, :, :] = shard[q][c, u, :, :]

    def pass_weights(q):
        for k, (arrived, owner) in enumerate(((straight[q], across[0]), (crossed[q], diagonal[0]))):
            arrived.wait_recv()
            piece = full[q].at[odd, owner]
            passed[q, k] = copies.start(piece, piece, neighbour)

    def column(row, lanes):
        return jnp.broadcast_to(row, (lanes, row.shape[1])).T

    def layer_norm():
        grid, tile = row_table.shape[0], 128
        images = lax.broadcasted_iota(jnp.int32, (128, count), 0)
        member = (jnp.broadcast_to(seg[...], (128, count)) == images).astype(f32)
        sizes = jnp.maximum(jnp.sum(member, axis=1, keepdims=True), 1.0)
        token_weight = jnp.sum(member * (1.0 / sizes), axis=0, keepdims=True)
        places = lax.broadcasted_iota(jnp.int32, (tile, 128), 1)
        for i in range(count // tile):
            span = slice(i * tile, (i + 1) * tile)
            own = pl.ds(pl.multiple_of(c * count + i * tile, tile), tile)
            embedded = tokens[span, :].astype(f32)
            for index, table in ((rows, row_table), (cols, col_table)):
                hot = column(index[:, span].astype(f32), 128)[:, :grid] == places[:, :grid].astype(f32)
                embedded += jnp.dot(
                    hot.astype(f32).astype(bf16), table[...], preferred_element_type=f32
                )
            average = jnp.mean(embedded, axis=1, keepdims=True)
            centered = embedded - average
            variance = jnp.mean(centered * centered, axis=1, keepdims=True)
            left = (centered * lax.rsqrt(variance + 1e-06) * gain[...].reshape(1, features)).astype(bf16)
            normed[own, :] = left
            norm_t[c, :, span] = left.T
            weight = column(token_weight[:, span], 128)[:, :1]
            right = (out_grad[span, :].astype(f32) * weight).astype(bf16)
            weighted[own, :] = right
            weight_t[c, :, span] = right.T
            for piece in (normed.at[own], weighted.at[own]):
                shared.append(copies.start(piece, piece, partner))

    def forward(q):
        near[q].wait_recv()
        for k in range(2):
            passed[q, k].wait_recv()
        tile = 256
        width = widths[q]
        total = CORES * count

        @pl.loop(0, total // tile)
        def _(i):
            own = pl.ds(pl.multiple_of(i * tile, tile), tile)
            v = jnp.dot(
                normed[own, :], full[q][0, :, :, :].reshape(features, width), preferred_element_type=f32
            )
            grad = jnp.dot(
                weighted[own, :], full[q][1, :, :, :].reshape(features, width), preferred_element_type=f32
            )
            square = v * v
            t = jnp.tanh(0.7978845608 * (v + 0.044715 * (square * v)))
            rising = 0.5 * (1.0 + t)
            slope = 0.7978845608 * (1.0 + 3.0 * 0.044715 * square)
            hidden[q][own, :] = (v * rising).astype(bf16)
            pre_grad[q][own, :] = (grad * (rising + 0.5 * v * (1.0 - t * t) * slope)).astype(bf16)

    def product(p, q, at_x, at_l):
        own = pl.ds(pl.multiple_of((at_x * PAIR + at_l) * block, 16), block)
        left, right = ((norm_t, pre_grad), (weight_t, hidden))[p]
        return sum(
            jnp.dot(
                left[k, own, :],
                right[q][k * count : (k + 1) * count, :],
                preferred_element_type=f32,
            )
            for k in range(CORES)
        )

    first, second, third, spread, beyond, last = {}, {}, {}, {}, {}, {}
    targets = (across, beside)

    def send_first(q):
        for slot in range(2):
            for p in range(PARTS):
                where = (1 - x, 1 - l) if slot == 0 else ((1 - x, l), (x, 1 - l))[p]
                s1[q][p, slot, :, :] = product(p, q, *where).astype(bf16)
                first[q, p, slot] = copies.start(
                    s1[q].at[p, slot], r1[q].at[p, slot], targets[p]
                )

    def send_second(q):
        for p in range(PARTS):
            own = product(p, q, *((x, 1 - l), (1 - x, l))[p])
            first[q, p, 0].wait_recv()
            s2[q][p, :, :] = (own + r1[q][p, 0, :, :].astype(f32)).astype(bf16)
            second[q, p] = copies.start(s2[q].at[p], r2[q].at[p], targets[1 - p])

    def send_third(q):
        for p in range(PARTS):
            own = product(p, q, x, l)
            first[q, p, 1].wait_recv()
            second[q, p].wait_recv()
            total = own + r1[q][p, 1, :, :].astype(f32) + r2[q][p, :, :].astype(f32)
            for level in range(levels):
                piece = total[level * deep : (level + 1) * deep]
                keep[q][level, p, :, :] = piece
                s3[q][level, p, :, :] = piece.astype(bf16)
        for k in range(1, levels):
            third[q, k] = copies.start(
                s3[q].at[ahead[k]], r3[q].at[h], above[k]
            )

    def send_whole(q):
        for k in range(1, levels):
            third[q, k].wait_recv()
        for p in range(PARTS):
            total = keep[q][h, p, :, :]
            for k in range(1, levels):
                total = total + r3[q][behind[k], p, :, :].astype(f32)
            whole[q][l, h, p, :, :] = total.astype(bf16)
            power = jnp.sum((total * total).reshape(deep // 8, 8, widths[q]), axis=0)
            for lane in range(widths[q] // 128):
                ss[...] += power[:, lane * 128 : (lane + 1) * 128]
        piece = whole[q].at[l, h]
        for k in range(1, levels):
            spread[q, k] = copies.start(piece, piece, above[k])
        beyond[q, 0] = copies.start(piece, piece, beside)

    def pass_whole(q):
        for k in range(1, levels):
            spread[q, k].wait_recv()
            piece = whole[q].at[l, behind[k]]
            beyond[q, k] = copies.start(piece, piece, beside)

    def send_last(q):
        for k in range(levels):
            beyond[q, k].wait_recv()
        last[q] = copies.start(
            whole[q].at[1 - c], out[q].at[c], partner
        )
        out[q][c, :, :, :, :] = whole[q][c, :, :, :, :]

    def add_squares():
        ss_s[0] = ss[...]
        waits = [copies.start(ss_s.at[0], ss_r.at[h], above[k]) for k in range(1, levels)]
        ss_r[h] = ss[...]
        yield
        for copy in waits:
            copy.wait_recv()
        running = ss_r[0]
        for level in range(1, levels):
            running = running + ss_r[level]
        for turn, target in enumerate((beside, across, partner)):
            ss_s[1 + turn] = running
            copy = copies.start(ss_s.at[1 + turn], ss_r.at[levels + turn], target)
            yield
            copy.wait_recv()
            running = running + ss_r[levels + turn]
        squares[...] = running

    ss[...] = jnp.zeros_like(ss)
    send_weights(0)
    send_weights(1)
    shared = []
    layer_norm()
    turned = [copies.start(piece, piece, partner) for piece in (norm_t.at[c], weight_t.at[c])]
    pass_weights(0)
    for copy in shared:
        copy.wait_recv()
    stages = forward, send_first, send_second, send_third, send_whole, pass_whole, send_last
    turns = add_squares()
    for tick in range(chunks + 5):
        if tick + 2 < chunks:
            send_weights(tick + 2)
        if tick + 1 < chunks:
            pass_weights(tick + 1)
        for stage, action in enumerate(stages):
            lag = max(stage - 1, 0)
            if 0 <= tick - lag < chunks:
                action(tick - lag)
            if tick == 0 and action is forward:
                for copy in turned:
                    copy.wait_recv()
        if tick >= chunks + 2:
            next(turns)
    for _ in turns:
        pass
    for q in range(chunks):
        last[q].wait_recv()
    copies.finish()


def update_kernel(
    entries, grads, squares, up, down, moment_up, moment_down, new_up, new_down, new_mu, new_md
):
    scale = lax.rsqrt(jnp.sum(squares[...]) / entries + 1e-06)
    end = 0
    for grad in grads:
        start, end = end, end + grad.shape[4]
        for p, old, moment, new, new_moment in (
            (0, up, moment_up, new_up, new_mu),
            (1, down, moment_down, new_down, new_md),
        ):
            fresh = momentum_keep * moment[:, start:end] + scale * grad[0, 0, p].astype(jnp.float32)
            new_moment[:, start:end] = fresh
            new[:, start:end] = old[:, start:end] - learn_rate * fresh


def cost(flops, moved):
    return pl.CostEstimate(flops=flops, bytes_accessed=moved, transcendentals=0)


def kernel_plan(
    tokens, out_grad, segments, pos_rows, pos_cols, row_table, col_table, norm_gain,
    master_up, master_down, moment_up, moment_down,
):
    bf16, f32 = jnp.bfloat16, jnp.float32
    shape = jax.ShapeDtypeStruct
    count, width = tokens.shape
    depth, hidden_units = master_up.shape
    gx, gy = lax.axis_size("gx"), lax.axis_size("gy")
    levels = gy // PAIR
    half = hidden_units // CORES
    both = CORES * count
    block = width // (gx // CORES) // PAIR
    deep = block // levels
    widths = chunk_widths(half)
    chunks = len(widths)

    def split(*lead):
        return [VMEM(lead + (w,), bf16) for w in widths]

    vm = pl.BlockSpec(memory_space=VMEM)
    n_copies = chunks * (11 + 2 * (levels - 1) + levels + 1) + count // 64 + levels + 4
    grads, squares = pl.pallas_call(
        block_kernel,
        out_shape=(
            [shape((CORES, levels, PARTS, deep, w), bf16) for w in widths],
            shape((8, 128), f32),
        ),
        in_specs=[vm] * 10,
        out_specs=([vm] * chunks, vm),
        scratch_shapes=[
            split(CORES, PARTS, depth),
            split(PARTS, gx, depth),
            VMEM((both, width), bf16),
            VMEM((both, width), bf16),
            VMEM((CORES, width, count), bf16),
            VMEM((CORES, width, count), bf16),
            split(both),
            split(both),
            split(PARTS, 2, block),
            split(PARTS, 2, block),
            split(PARTS, block),
            split(PARTS, block),
            split(levels, PARTS, deep),
            split(levels, PARTS, deep),
            [VMEM((levels, PARTS, deep, w), f32) for w in widths],
            split(PAIR, levels, PARTS, deep),
            VMEM((8, 128), f32),
            VMEM((4, 8, 128), f32),
            VMEM((levels + 3, 8, 128), f32),
            pltpu.SemaphoreType.DMA((n_copies,)),
            pltpu.SemaphoreType.DMA((n_copies,)),
        ],
        cost_estimate=cost(8 * both * width * half, 8 * both * width),
        compiler_params=pltpu.CompilerParams(
            collective_id=0, has_side_effects=True, vmem_limit_bytes=VMEM_LIMIT
        ),
    )(
        master_up,
        master_down,
        tokens,
        out_grad,
        segments,
        pos_rows.reshape(1, count),
        pos_cols.reshape(1, count),
        row_table,
        col_table,
        norm_gain,
    )

    flat = pl.BlockSpec((deep, half), lambda i, j: (i, j))
    return pl.pallas_call(
        functools.partial(update_kernel, 2.0 * width * hidden_units),
        grid=(levels, CORES),
        out_shape=(shape(master_up.shape, f32),) * 4,
        in_specs=[
            [
                pl.BlockSpec((1, 1, PARTS, deep, w), lambda i, j: (j, i, 0, 0, 0))
                for w in widths
            ],
            pl.BlockSpec((8, 128), lambda i, j: (0, 0)),
            flat, flat, flat, flat,
        ],
        out_specs=(flat,) * 4,
        cost_estimate=cost(8 * master_up.size, 34 * master_up.size),
        compiler_params=pltpu.CompilerParams(vmem_limit_bytes=VMEM_LIMIT),
    )(grads, squares, master_up, master_down, moment_up, moment_down)


def table_lookup(positions, table):
    onehot = (
        positions[:, None] == jnp.arange(table.shape[0], dtype=jnp.int32)[None, :]
    ).astype(jnp.bfloat16)
    return jnp.dot(onehot, table, preferred_element_type=jnp.float32)


def column_product(left, right):
    return lax.dot_general(
        left, right, (((0,), (0,)), ((), ())), preferred_element_type=jnp.float32
    )


def collective_plan(
    tokens, out_grad, segments, pos_rows, pos_cols, row_table, col_table, norm_gain,
    master_up, master_down, moment_up, moment_down,
):
    images = 8
    embedded = (
        tokens.astype(jnp.float32)
        + table_lookup(pos_rows, row_table)
        + table_lookup(pos_cols, col_table)
    )
    average = jnp.mean(embedded, axis=1, keepdims=True)
    centered = embedded - average
    variance = jnp.mean(centered * centered, axis=1, keepdims=True)
    normed = (centered * lax.rsqrt(variance + 1e-06) * norm_gain[None, :]).astype(jnp.bfloat16)
    member = (segments[0][:, None] == jnp.arange(images, dtype=jnp.int32)[None, :]).astype(
        jnp.float32
    )
    token_weight = jnp.dot(member, 1.0 / jnp.sum(member, axis=0))
    weighted = (out_grad.astype(jnp.float32) * token_weight[:, None]).astype(jnp.bfloat16)
    w_up = lax.all_gather(master_up.astype(jnp.bfloat16), "gx", axis=0, tiled=True)
    pre_act = jnp.dot(normed, w_up, preferred_element_type=jnp.float32)
    hidden, backward = jax.vjp(gelu_tanh, pre_act)
    w_down = lax.all_gather(master_down.astype(jnp.bfloat16), "gx", axis=0, tiled=True)
    hidden_grad = jnp.dot(weighted, w_down, preferred_element_type=jnp.float32)
    pre_grad = backward(hidden_grad)[0].astype(jnp.bfloat16)
    grads = [column_product(normed, pre_grad), column_product(weighted, hidden.astype(jnp.bfloat16))]
    group_sum = lax.psum_scatter(
        jnp.concatenate(grads, axis=1).astype(jnp.bfloat16), "gx", scatter_dimension=0, tiled=True
    )
    grad_sum = lax.psum(group_sum, "gy").astype(jnp.float32)
    squares = lax.psum(jnp.sum(grad_sum * grad_sum), "gx")
    entries = 2.0 * tokens.shape[1] * master_up.shape[1]
    scale = lax.rsqrt(squares / entries + 1e-06)
    half = master_up.shape[1]
    new_mu = momentum_keep * moment_up + scale * grad_sum[:, :half]
    new_md = momentum_keep * moment_down + scale * grad_sum[:, half:]
    return master_up - learn_rate * new_mu, master_down - learn_rate * new_md, new_mu, new_md


def solution(mesh):
    gx, gy = mesh.shape["gx"], mesh.shape["gy"]

    def on_device(*args):
        width, half = args[0].shape[1], args[8].shape[1] // CORES
        fits = (
            gx == 2 * CORES
            and gy % PAIR == 0
            and gy > PAIR
            and args[0].shape[0] % 128 == 0
            and width % (gx * gy // CORES * 16) == 0
            and width % (gx * 16) == 0
            and gy // PAIR % 2 == 0
            and half % 128 == 0
        )
        return (kernel_plan if fits else collective_plan)(*args)

    both, rows = P(("gx", "gy"), None), P("gx", None)
    return jax.shard_map(
        on_device,
        mesh=mesh,
        in_specs=(both, both, both, P(("gx", "gy")), P(("gx", "gy")), P(), P(), P())
        + (rows,) * 4,
        out_specs=(rows,) * 4,
        check_vma=False,
    )
```

```python
import functools

import jax
import jax.numpy as jnp
from jax import lax
from jax.experimental import pallas as pl
from jax.experimental.pallas import tpu as pltpu
from jax.sharding import PartitionSpec as P

momentum_keep = 0.9
learn_rate = 0.01
MESH = pl.DeviceIdType.MESH
VMEM = pltpu.VMEM
VMEM_LIMIT = 60 * 1024 * 1024
CORES = 2
PAIR = 2
PARTS = 2


def gelu_tanh(values):
    return (
        0.5
        * values
        * (1.0 + jnp.tanh(0.7978845608 * (values + 0.044715 * values * values * values)))
    )


def chunk_widths(columns):
    if columns % 256 or columns < 768:
        return [128] * (columns // 128)
    return [128] * 2 + [256] * (columns // 256 - 2) + [128] * 2


class Copies:
    def __init__(self, send, recv):
        self.send, self.recv, self.count, self.all = send, recv, 0, []

    def start(self, src, dst, device):
        copy = pltpu.make_async_remote_copy(
            src_ref=src,
            dst_ref=dst,
            send_sem=self.send.at[self.count],
            recv_sem=self.recv.at[self.count],
            device_id=device,
            device_id_type=MESH,
        )
        copy.start()
        self.count += 1
        self.all.append(copy)
        return copy

    def finish(self):
        for copy in self.all:
            copy.wait_send()


def greet(devices):
    barrier = pltpu.get_barrier_semaphore()
    for device in devices:
        pl.semaphore_signal(barrier, inc=1, device_id=device, device_id_type=MESH)
    pl.semaphore_wait(barrier, len(devices))


def place():
    gx, gy = lax.axis_index("gx"), lax.axis_index("gy")
    return gx, gy, gx // CORES, lax.rem(gx, CORES), gy // PAIR, lax.rem(gy, PAIR)


def block_kernel(
    up_home, down_home, tokens, out_grad, seg, rows, cols, row_table, col_table, gain,
    out, squares,
    shard, full, normed, weighted, norm_t, weight_t, pre_grad, hidden,
    s1, r1, s2, r2, s3, r3, keep, whole, ss, ss_s, ss_r, master_up, master_down, fetch, send, recv,
):
    bf16, f32 = jnp.bfloat16, jnp.float32
    gx, gy, x, c, h, l = place()
    levels = lax.axis_size("gy") // PAIR
    partner = (x * CORES + 1 - c, gy)
    across = ((1 - x) * CORES + c, gy)
    diagonal = ((1 - x) * CORES + 1 - c, gy)
    beside = (gx, h * PAIR + 1 - l)
    odd = lax.rem(h, 2)
    neighbour = (gx, (h + 1 - 2 * odd) * PAIR + l)
    ahead = [lax.rem(h + k, levels) for k in range(levels)]
    behind = [lax.rem(h + levels - k, levels) for k in range(levels)]
    above = [(gx, ahead[k] * PAIR + l) for k in range(levels)]
    half = master_up.shape[1] // CORES
    widths = [piece.shape[3] for piece in shard]
    chunks = len(widths)
    early = widths[0] + widths[1]
    fetched = []
    for lo, hi in ((0, early), (early, half)):
        for k in range(CORES):
            for home, here in ((up_home, master_up), (down_home, master_down)):
                span = pl.ds(k * half + lo, hi - lo)
                copy = pltpu.make_async_copy(
                    home.at[:, span], here.at[:, span], fetch.at[len(fetched)]
                )
                copy.start()
                fetched.append(copy)
    greet([partner, across, diagonal, beside] + above[1:])
    copies = Copies(send, recv)
    offset = [sum(widths[:q]) for q in range(chunks)]
    count, features = tokens.shape
    block = s1[0].shape[2]
    deep = block // levels

    straight, crossed, near, passed = {}, {}, {}, {}

    def send_weights(q):
        for k in range(CORES):
            start = k * half + offset[q]
            shard[q][k, 0, :, :] = master_up[:, start : start + widths[q]].astype(bf16)
            shard[q][k, 1, :, :] = master_down[:, start : start + widths[q]].astype(bf16)
        mine = full[q].at[odd, gx]
        straight[q] = copies.start(shard[q].at[c, odd], mine, across)
        crossed[q] = copies.start(shard[q].at[1 - c, odd], mine, diagonal)
        near[q] = copies.start(
            shard[q].at[1 - c], full[q].at[:, gx], partner
        )
        for u in range(PARTS):
            full[q][u, gx, :, :] = shard[q][c, u, :, :]

    def pass_weights(q):
        for k, (arrived, owner) in enumerate(((straight[q], across[0]), (crossed[q], diagonal[0]))):
            arrived.wait_recv()
            piece = full[q].at[odd, owner]
            passed[q, k] = copies.start(piece, piece, neighbour)

    def column(row, lanes):
        return jnp.broadcast_to(row, (lanes, row.shape[1])).T

    def layer_norm():
        grid, tile = row_table.shape[0], 128
        images = lax.broadcasted_iota(jnp.int32, (128, count), 0)
        member = (jnp.broadcast_to(seg[...], (128, count)) == images).astype(f32)
        sizes = jnp.maximum(jnp.sum(member, axis=1, keepdims=True), 1.0)
        token_weight = jnp.sum(member * (1.0 / sizes), axis=0, keepdims=True)
        places = lax.broadcasted_iota(jnp.int32, (tile, 128), 1)
        for i in range(count // tile):
            span = slice(i * tile, (i + 1) * tile)
            own = pl.ds(pl.multiple_of(c * count + i * tile, tile), tile)
            embedded = tokens[span, :].astype(f32)
            for index, table in ((rows, row_table), (cols, col_table)):
                hot = column(index[:, span].astype(f32), 128)[:, :grid] == places[:, :grid].astype(f32)
                embedded += jnp.dot(
                    hot.astype(f32).astype(bf16), table[...], preferred_element_type=f32
                )
            average = jnp.mean(embedded, axis=1, keepdims=True)
            centered = embedded - average
            variance = jnp.mean(centered * centered, axis=1, keepdims=True)
            left = (centered * lax.rsqrt(variance + 1e-06) * gain[...].reshape(1, features)).astype(bf16)
            normed[own, :] = left
            norm_t[c, :, span] = left.T
            weight = column(token_weight[:, span], 128)[:, :1]
            right = (out_grad[span, :].astype(f32) * weight).astype(bf16)
            weighted[own, :] = right
            weight_t[c, :, span] = right.T
            for piece in (normed.at[own], weighted.at[own]):
                shared.append(copies.start(piece, piece, partner))

    def forward(q):
        near[q].wait_recv()
        for k in range(2):
            passed[q, k].wait_recv()
        tile = 256
        width = widths[q]
        total = CORES * count

        @pl.loop(0, total // tile)
        def _(i):
            own = pl.ds(pl.multiple_of(i * tile, tile), tile)
            v = jnp.dot(
                normed[own, :], full[q][0, :, :, :].reshape(features, width), preferred_element_type=f32
            )
            grad = jnp.dot(
                weighted[own, :], full[q][1, :, :, :].reshape(features, width), preferred_element_type=f32
            )
            square = v * v
            t = jnp.tanh(0.7978845608 * (v + 0.044715 * (square * v)))
            rising = 0.5 * (1.0 + t)
            slope = 0.7978845608 * (1.0 + 3.0 * 0.044715 * square)
            hidden[q][own, :] = (v * rising).astype(bf16)
            pre_grad[q][own, :] = (grad * (rising + 0.5 * v * (1.0 - t * t) * slope)).astype(bf16)

    def product(p, q, at_x, at_l):
        own = pl.ds(pl.multiple_of((at_x * PAIR + at_l) * block, 16), block)
        left, right = ((norm_t, pre_grad), (weight_t, hidden))[p]
        return sum(
            jnp.dot(
                left[k, own, :],
                right[q][k * count : (k + 1) * count, :],
                preferred_element_type=f32,
            )
            for k in range(CORES)
        )

    first, second, third, spread, beyond, last = {}, {}, {}, {}, {}, {}
    targets = (across, beside)

    def send_first(q):
        for slot in range(2):
            for p in range(PARTS):
                where = (1 - x, 1 - l) if slot == 0 else ((1 - x, l), (x, 1 - l))[p]
                s1[q][p, slot, :, :] = product(p, q, *where).astype(bf16)
                first[q, p, slot] = copies.start(
                    s1[q].at[p, slot], r1[q].at[p, slot], targets[p]
                )

    def send_second(q):
        for p in range(PARTS):
            own = product(p, q, *((x, 1 - l), (1 - x, l))[p])
            first[q, p, 0].wait_recv()
            s2[q][p, :, :] = (own + r1[q][p, 0, :, :].astype(f32)).astype(bf16)
            second[q, p] = copies.start(s2[q].at[p], r2[q].at[p], targets[1 - p])

    def send_third(q):
        for p in range(PARTS):
            own = product(p, q, x, l)
            first[q, p, 1].wait_recv()
            second[q, p].wait_recv()
            total = own + r1[q][p, 1, :, :].astype(f32) + r2[q][p, :, :].astype(f32)
            for level in range(levels):
                piece = total[level * deep : (level + 1) * deep]
                keep[q][level, p, :, :] = piece
                s3[q][level, p, :, :] = piece.astype(bf16)
        for k in range(1, levels):
            third[q, k] = copies.start(
                s3[q].at[ahead[k]], r3[q].at[h], above[k]
            )

    def send_whole(q):
        for k in range(1, levels):
            third[q, k].wait_recv()
        for p in range(PARTS):
            total = keep[q][h, p, :, :]
            for k in range(1, levels):
                total = total + r3[q][behind[k], p, :, :].astype(f32)
            whole[q][l, h, p, :, :] = total.astype(bf16)
            power = jnp.sum((total * total).reshape(deep // 8, 8, widths[q]), axis=0)
            for lane in range(widths[q] // 128):
                ss[...] += power[:, lane * 128 : (lane + 1) * 128]
        piece = whole[q].at[l, h]
        for k in range(1, levels):
            spread[q, k] = copies.start(piece, piece, above[k])
        beyond[q, 0] = copies.start(piece, piece, beside)

    def pass_whole(q):
        for k in range(1, levels):
            spread[q, k].wait_recv()
            piece = whole[q].at[l, behind[k]]
            beyond[q, k] = copies.start(piece, piece, beside)

    def send_last(q):
        for k in range(levels):
            beyond[q, k].wait_recv()
        last[q] = copies.start(
            whole[q].at[1 - c], out[q].at[c], partner
        )
        out[q][c, :, :, :, :] = whole[q][c, :, :, :, :]

    def add_squares():
        ss_s[0] = ss[...]
        waits = [copies.start(ss_s.at[0], ss_r.at[h], above[k]) for k in range(1, levels)]
        ss_r[h] = ss[...]
        yield
        for copy in waits:
            copy.wait_recv()
        running = ss_r[0]
        for level in range(1, levels):
            running = running + ss_r[level]
        for turn, target in enumerate((beside, across, partner)):
            ss_s[1 + turn] = running
            copy = copies.start(ss_s.at[1 + turn], ss_r.at[levels + turn], target)
            yield
            copy.wait_recv()
            running = running + ss_r[levels + turn]
        squares[...] = running

    ss[...] = jnp.zeros_like(ss)
    for copy in fetched[: 2 * CORES]:
        copy.wait()
    send_weights(0)
    send_weights(1)
    for copy in fetched[2 * CORES :]:
        copy.wait()
    shared = []
    layer_norm()
    turned = [copies.start(piece, piece, partner) for piece in (norm_t.at[c], weight_t.at[c])]
    pass_weights(0)
    for copy in shared:
        copy.wait_recv()
    stages = forward, send_first, send_second, send_third, send_whole, pass_whole, send_last
    turns = add_squares()
    for tick in range(chunks + 5):
        if tick + 2 < chunks:
            send_weights(tick + 2)
        if tick + 1 < chunks:
            pass_weights(tick + 1)
        for stage, action in enumerate(stages):
            lag = max(stage - 1, 0)
            if 0 <= tick - lag < chunks:
                action(tick - lag)
            if tick == 0 and action is forward:
                for copy in turned:
                    copy.wait_recv()
        if tick >= chunks + 2:
            next(turns)
    for _ in turns:
        pass
    for q in range(chunks):
        last[q].wait_recv()
    copies.finish()


def update_kernel(
    entries, grads, squares, up, down, moment_up, moment_down, new_up, new_down, new_mu, new_md
):
    scale = lax.rsqrt(jnp.sum(squares[...]) / entries + 1e-06)
    end = 0
    for grad in grads:
        start, end = end, end + grad.shape[4]
        for p, old, moment, new, new_moment in (
            (0, up, moment_up, new_up, new_mu),
            (1, down, moment_down, new_down, new_md),
        ):
            fresh = momentum_keep * moment[:, start:end] + scale * grad[0, 0, p].astype(jnp.float32)
            new_moment[:, start:end] = fresh
            new[:, start:end] = old[:, start:end] - learn_rate * fresh


def cost(flops, moved):
    return pl.CostEstimate(flops=flops, bytes_accessed=moved, transcendentals=0)


def kernel_plan(
    tokens, out_grad, segments, pos_rows, pos_cols, row_table, col_table, norm_gain,
    master_up, master_down, moment_up, moment_down,
):
    bf16, f32 = jnp.bfloat16, jnp.float32
    shape = jax.ShapeDtypeStruct
    count, width = tokens.shape
    depth, hidden_units = master_up.shape
    gx, gy = lax.axis_size("gx"), lax.axis_size("gy")
    levels = gy // PAIR
    half = hidden_units // CORES
    both = CORES * count
    block = width // (gx // CORES) // PAIR
    deep = block // levels
    widths = chunk_widths(half)
    chunks = len(widths)

    def split(*lead):
        return [VMEM(lead + (w,), bf16) for w in widths]

    vm = pl.BlockSpec(memory_space=VMEM)
    n_copies = chunks * (11 + 2 * (levels - 1) + levels + 1) + count // 64 + levels + 4
    grads, squares = pl.pallas_call(
        block_kernel,
        out_shape=(
            [shape((CORES, levels, PARTS, deep, w), bf16) for w in widths],
            shape((8, 128), f32),
        ),
        in_specs=[pl.BlockSpec(memory_space=pl.ANY)] * 2 + [vm] * 8,
        out_specs=([vm] * chunks, vm),
        scratch_shapes=[
            split(CORES, PARTS, depth),
            split(PARTS, gx, depth),
            VMEM((both, width), bf16),
            VMEM((both, width), bf16),
            VMEM((CORES, width, count), bf16),
            VMEM((CORES, width, count), bf16),
            split(both),
            split(both),
            split(PARTS, 2, block),
            split(PARTS, 2, block),
            split(PARTS, block),
            split(PARTS, block),
            split(levels, PARTS, deep),
            split(levels, PARTS, deep),
            [VMEM((levels, PARTS, deep, w), f32) for w in widths],
            split(PAIR, levels, PARTS, deep),
            VMEM((8, 128), f32),
            VMEM((4, 8, 128), f32),
            VMEM((levels + 3, 8, 128), f32),
            VMEM(master_up.shape, f32),
            VMEM(master_down.shape, f32),
            pltpu.SemaphoreType.DMA((4 * CORES,)),
            pltpu.SemaphoreType.DMA((n_copies,)),
            pltpu.SemaphoreType.DMA((n_copies,)),
        ],
        cost_estimate=cost(8 * both * width * half, 8 * both * width),
        compiler_params=pltpu.CompilerParams(
            collective_id=0, has_side_effects=True, vmem_limit_bytes=VMEM_LIMIT
        ),
    )(
        master_up,
        master_down,
        tokens,
        out_grad,
        segments,
        pos_rows.reshape(1, count),
        pos_cols.reshape(1, count),
        row_table,
        col_table,
        norm_gain,
    )

    flat = pl.BlockSpec((deep, half), lambda i, j: (i, j))
    return pl.pallas_call(
        functools.partial(update_kernel, 2.0 * width * hidden_units),
        grid=(levels, CORES),
        out_shape=(shape(master_up.shape, f32),) * 4,
        in_specs=[
            [
                pl.BlockSpec((1, 1, PARTS, deep, w), lambda i, j: (j, i, 0, 0, 0))
                for w in widths
            ],
            pl.BlockSpec((8, 128), lambda i, j: (0, 0)),
            flat, flat, flat, flat,
        ],
        out_specs=(flat,) * 4,
        cost_estimate=cost(8 * master_up.size, 34 * master_up.size),
        compiler_params=pltpu.CompilerParams(vmem_limit_bytes=VMEM_LIMIT),
    )(grads, squares, master_up, master_down, moment_up, moment_down)


def table_lookup(positions, table):
    onehot = (
        positions[:, None] == jnp.arange(table.shape[0], dtype=jnp.int32)[None, :]
    ).astype(jnp.bfloat16)
    return jnp.dot(onehot, table, preferred_element_type=jnp.float32)


def column_product(left, right):
    return lax.dot_general(
        left, right, (((0,), (0,)), ((), ())), preferred_element_type=jnp.float32
    )


def collective_plan(
    tokens, out_grad, segments, pos_rows, pos_cols, row_table, col_table, norm_gain,
    master_up, master_down, moment_up, moment_down,
):
    images = 8
    embedded = (
        tokens.astype(jnp.float32)
        + table_lookup(pos_rows, row_table)
        + table_lookup(pos_cols, col_table)
    )
    average = jnp.mean(embedded, axis=1, keepdims=True)
    centered = embedded - average
    variance = jnp.mean(centered * centered, axis=1, keepdims=True)
    normed = (centered * lax.rsqrt(variance + 1e-06) * norm_gain[None, :]).astype(jnp.bfloat16)
    member = (segments[0][:, None] == jnp.arange(images, dtype=jnp.int32)[None, :]).astype(
        jnp.float32
    )
    token_weight = jnp.dot(member, 1.0 / jnp.sum(member, axis=0))
    weighted = (out_grad.astype(jnp.float32) * token_weight[:, None]).astype(jnp.bfloat16)
    w_up = lax.all_gather(master_up.astype(jnp.bfloat16), "gx", axis=0, tiled=True)
    pre_act = jnp.dot(normed, w_up, preferred_element_type=jnp.float32)
    hidden, backward = jax.vjp(gelu_tanh, pre_act)
    w_down = lax.all_gather(master_down.astype(jnp.bfloat16), "gx", axis=0, tiled=True)
    hidden_grad = jnp.dot(weighted, w_down, preferred_element_type=jnp.float32)
    pre_grad = backward(hidden_grad)[0].astype(jnp.bfloat16)
    grads = [column_product(normed, pre_grad), column_product(weighted, hidden.astype(jnp.bfloat16))]
    group_sum = lax.psum_scatter(
        jnp.concatenate(grads, axis=1).astype(jnp.bfloat16), "gx", scatter_dimension=0, tiled=True
    )
    grad_sum = lax.psum(group_sum, "gy").astype(jnp.float32)
    squares = lax.psum(jnp.sum(grad_sum * grad_sum), "gx")
    entries = 2.0 * tokens.shape[1] * master_up.shape[1]
    scale = lax.rsqrt(squares / entries + 1e-06)
    half = master_up.shape[1]
    new_mu = momentum_keep * moment_up + scale * grad_sum[:, :half]
    new_md = momentum_keep * moment_down + scale * grad_sum[:, half:]
    return master_up - learn_rate * new_mu, master_down - learn_rate * new_md, new_mu, new_md


def solution(mesh):
    gx, gy = mesh.shape["gx"], mesh.shape["gy"]

    def on_device(*args):
        width, half = args[0].shape[1], args[8].shape[1] // CORES
        fits = (
            gx == 2 * CORES
            and gy % PAIR == 0
            and gy > PAIR
            and args[0].shape[0] % 128 == 0
            and width % (gx * gy // CORES * 16) == 0
            and width % (gx * 16) == 0
            and gy // PAIR % 2 == 0
            and half % 128 == 0
        )
        return (kernel_plan if fits else collective_plan)(*args)

    both, rows = P(("gx", "gy"), None), P("gx", None)
    return jax.shard_map(
        on_device,
        mesh=mesh,
        in_specs=(both, both, both, P(("gx", "gy")), P(("gx", "gy")), P(), P(), P())
        + (rows,) * 4,
        out_specs=(rows,) * 4,
        check_vma=False,
    )
```
